128 devices in a mesh: gx: 4 (over x), gy: 32 (over z, y, core).
Axes of the slice: x: 4, y: 4, z: 4, core: 2. Of those that a mesh axis runs over, the one named last changes fastest.
Arguments:
- fine_feat: bfloat16 [4, 32, 16, 128, 256], P('gx', 'gy'), may hold values from -6 to 6
- coarse_grad: bfloat16 [4, 32, 4, 128, 256], P('gx', 'gy'), may hold values from -6 to 6
- kernel_map: int32 [4, 32, 27, 16], P('gx', 'gy'), may hold values from 0 to 36, as said below
- counts: int32 [4, 32], P('gx', 'gy'), may hold values from 4 to 16, as said below
- weight: bfloat16 [27, 256, 256], replicated, may hold values from -0.078125 to 0.078125
Outputs:
- fine_grad: bfloat16 [4, 32, 16, 128, 256], P('gx', 'gy')
- weight_grad: float32 [6912, 256], P(('gx', 'gy'))
The draws below stay inside these ranges and needn't reach their ends.
Inputs may be any that keep to these rules, and one draw needn't show every extreme that they name: `kernel_map`: an entry v < 36 names coarse block v % 4 of the partition offset by (v // 4) // 3 - 1 along gx and (v // 4) % 3 - 1 along gy; 36 names no block. Entries of unoccupied slots are arbitrary. `counts`: fine block slots at or beyond a partition's count are unoccupied and their features are arbitrary.
All inputs are finite; a program needn't handle non-finite values.
Results may differ from the reference program's by a relative error of at most 0.001.
Values may be sent and summed in bfloat16 or wider, within the bound.
A program may use at most 128 MiB of HBM per device.

```python
import math
import jax
import jax.numpy as jnp
from jax import lax

C = 256
BLOCK = 128
K = 27
FB_DEV = 16
CB_DEV = 4
VOXELS = 262144
N_GX = 4
N_GY = 32


def draw_kernel_map(key, part):
    key = jax.random.fold_in(key, 11)
    first, second, third = jax.random.split(key, 3)
    shape = (N_GX, N_GY, K, FB_DEV)
    region = jax.random.randint(first, shape, 0, 9)
    within = jax.random.randint(second, shape, 0, CB_DEV)
    vacant = jax.random.randint(third, shape, 0, 8) == 0
    values = jnp.where(vacant, 9 * CB_DEV, region * CB_DEV + within)
    values = values.at[:, :, 0, 0].set(9 * CB_DEV)
    values = values.at[:, :, 1, 0].set(0)
    return values.astype(jnp.int32)


def draw_counts(key, part):
    key = jax.random.fold_in(key, 12)
    first, second = jax.random.split(key, 2)
    values = jax.random.randint(first, (N_GX * N_GY,), FB_DEV // 4, FB_DEV + 1)
    chosen = jax.random.randint(second, (), 0, N_GX * N_GY)
    values = values.at[chosen].set(FB_DEV)
    return values.reshape(N_GX, N_GY).astype(jnp.int32)


def shard_levels(own_key, extent, cuts, low, high):
    level, own = 1.0, jax.random.fold_in(own_key, 6)
    for axis_at, shards_of in cuts:
        draws = jnp.exp(jax.random.uniform(jax.random.fold_in(own, axis_at), (shards_of,), jnp.float32, low / len(cuts), high / len(cuts)))
        level = level * jnp.repeat(draws, extent[axis_at] // shards_of).reshape([-1 if axis == axis_at else 1 for axis in range(len(extent))])
    return level


def centred(stream_key, extent, deviation, bound, shards=(), kind=jnp.bfloat16):
    values = jax.random.normal(stream_key, extent, jnp.float32) * deviation
    if len(shards) > 0:
        values = shard_levels(stream_key, extent, shards, -0.22, 0.18) * values
    return jnp.clip(values, min=-bound, max=bound).astype(kind)


def setup_inputs(seed: int = 0) -> dict:
    keys = jax.random.split(jax.random.key(seed), 6)
    return {
        "fine_feat": centred(keys[0], (N_GX, N_GY, FB_DEV, BLOCK, C), 1.0, 6.0, ((0, 4), (1, 32))),
        "coarse_grad": centred(keys[1], (N_GX, N_GY, CB_DEV, BLOCK, C), 1.0, 6.0, ((0, 4), (1, 32))),
        "kernel_map": draw_kernel_map(jax.random.fold_in(keys[5], 71), 0),
        "counts": draw_counts(jax.random.fold_in(keys[5], 71), 0),
        "weight": centred(keys[4], (K, C, C), (K * C) ** -0.5, 0.078125),
    }


def reference(fine_feat, coarse_grad, kernel_map, counts, weight):
    padded = jnp.pad(coarse_grad, ((1, 1), (1, 1), (0, 0), (0, 0), (0, 0)))
    weight_full = weight.astype(jnp.float32)
    factor = 1.0 / math.sqrt(VOXELS)
    slots = jnp.arange(FB_DEV, dtype=jnp.int32)

    def one_part(carried, position):
        row_pos = (position // N_GY).astype(jnp.int32)
        col_pos = (position % N_GY).astype(jnp.int32)
        zero_index = jnp.zeros((), jnp.int32)
        beside_all = lax.dynamic_slice(padded, (row_pos, col_pos, zero_index, zero_index, zero_index), (3, 3, CB_DEV, BLOCK, C))
        coarse_pool = jnp.concatenate([beside_all.reshape(9 * CB_DEV, BLOCK, C), jnp.zeros((1, BLOCK, C), jnp.bfloat16)], axis=0)
        offsets_map = kernel_map[row_pos, col_pos]
        occupied = (slots < counts[row_pos, col_pos]).astype(jnp.float32)
        gathered = coarse_pool[offsets_map].astype(jnp.float32)
        grad_in = jnp.einsum('kbvo,kio->bvi', gathered, weight_full) * occupied[:, None, None]
        fine_rows = fine_feat[row_pos, col_pos].astype(jnp.float32) * occupied[:, None, None]
        partial_sum = jnp.einsum('bvi,kbvo->kio', fine_rows, gathered) * jnp.float32(factor)
        return (carried + partial_sum, grad_in.astype(jnp.bfloat16))
    total, grads = lax.scan(one_part, jnp.zeros((K, C, C), jnp.float32), jnp.arange(N_GX * N_GY, dtype=jnp.int32))
    fine_grad = grads.reshape(N_GX, N_GY, FB_DEV, BLOCK, C)
    return (fine_grad, total.reshape(K * C, C))
```

```python
import functools
import math

import jax
import jax.numpy as jnp
from jax import lax
from jax.experimental import pallas as pl
from jax.experimental.pallas import tpu as pltpu
from jax.sharding import PartitionSpec as P

MESH = pl.DeviceIdType.MESH
F32, BF16, I16 = jnp.float32, jnp.bfloat16, jnp.int16
K, C, BLOCK, SLOTS, COARSE = 27, 256, 128, 16, 4
HALF = C // 2
GROUPS, PER_GROUP = 3, 9
PIECES, PIECE = 16, 432
LONG = PIECE + 16
YROWS = 128
YLONG = YROWS + 16
MINE = 54
LEVELS = 32767.0

dot = functools.partial(jnp.dot, preferred_element_type=F32)


def encode(values):
    top = jnp.maximum(jnp.max(jnp.abs(values), axis=0, keepdims=True), 1e-35)
    power = jnp.ceil(jnp.log2(top) + 1e-3)
    codes = jnp.floor(values * (jnp.exp2(-power) * LEVELS) + 0.5).astype(jnp.int32)
    return codes.astype(I16), jnp.broadcast_to(power, (16, HALF)).astype(jnp.int32).astype(I16)


def decode(ref, rows):
    power = ref[rows : rows + 16, :].astype(jnp.int32).astype(F32)[0:1, :]
    return ref[0:rows, :].astype(jnp.int32).astype(F32) * (jnp.exp2(power) * (1.0 / LEVELS))


def kernel(
    fine_hbm, coarse_hbm, map_ref, counts_ref, weight_hbm,
    fine_out, weight_out,
    pool, fine_in, fine_t, weight_in, weight_t, acc, from_mate,
    send1, recv1, total1, send2, recv2, total2, send3, recv3, total3,
    own_rows, mate_rows, fine_vmem, weight_vmem,
    load_sem, hx_send, hx_recv, hy_send, hy_recv, m_send, m_recv,
    s1_send, s1_recv, s2_send, s2_recv, s3_send, s3_recv, f_sem,
    out_sem,
):
    gx, gy = lax.axis_index("gx"), lax.axis_index("gy")
    z, y, c = gy // 8, (gy // 2) % 4, gy % 2

    def at(x_, z_, y_, c_):
        return (x_, z_ * 8 + y_ * 2 + c_)

    mate = at(gx, z, y, 1 - c)
    up, down = (gx, (gy + 1) % 32), (gx, (gy + 31) % 32)
    away = (gx, (gy + jnp.where(c == 0, 31, 1)) % 32)

    loads = [
        pltpu.make_async_copy(coarse_hbm, pool.at[16:20], load_sem.at[0]),
        pltpu.make_async_copy(fine_hbm, fine_in, load_sem.at[1]),
        pltpu.make_async_copy(weight_hbm, weight_in, load_sem.at[2]),
    ]
    for copy in loads:
        copy.start()

    barrier = pltpu.get_barrier_semaphore()
    partners = [mate, away]
    for d in (1, 2, 3):
        partners += [at((gx + d) % 4, z, y, c), at(gx, (z + d) % 4, y, c), at(gx, z, (y + d) % 4, c)]
    for who in partners:
        pl.semaphore_signal(barrier, inc=1, device_id=who, device_id_type=MESH)
    pl.semaphore_wait(barrier, len(partners))

    def remote(src, dst, send, recv, who):
        return pltpu.make_async_remote_copy(
            src_ref=src, dst_ref=dst, send_sem=send, recv_sem=recv, device_id=who, device_id_type=MESH
        )

    def region(r):
        return pool.at[4 * r : 4 * r + 4]

    halo = []
    for i, (who, r) in enumerate(((((gx + 1) % 4, gy), 1), (((gx + 3) % 4, gy), 7))):
        copy = remote(coarse_hbm, region(r), hx_send.at[i], hx_recv.at[i], who)
        copy.start()
        halo.append(copy)

    def along_y(p, src):
        for i, (who, q) in enumerate(((up, 0), (down, 2))):
            copy = remote(src, region(3 * p + q), hy_send.at[i, p], hy_recv.at[i, p], who)
            copy.start()
            halo_y.append(copy)

    halo_y = []
    along_y(1, coarse_hbm)

    pool[36] = jnp.zeros((BLOCK, C), BF16)
    count = counts_ref[0, 0]
    loads[1].wait()
    for f in range(SLOTS):
        block = jnp.where(f < count, fine_in[f], jnp.zeros((), BF16))
        fine_t[:, f * BLOCK : (f + 1) * BLOCK] = block.T

    halo[0].wait_recv()
    along_y(0, region(1))
    halo[1].wait_recv()
    along_y(2, region(7))
    loads[2].wait()

    def turn(k, carry):
        weight_t[pl.ds(pl.multiple_of(k * C, C), C), :] = weight_in[k].T
        return carry

    lax.fori_loop(0, K, turn, 0)
    loads[0].wait()
    for copy in halo:
        copy.wait_send()
    for copy in halo_y:
        copy.wait()

    @pl.when(gx == 0)
    def _():
        pool[0:12] = jnp.zeros((12, BLOCK, C), BF16)

    @pl.when(gx == 3)
    def _():
        pool[24:36] = jnp.zeros((12, BLOCK, C), BF16)

    for edge, q in ((0, 0), (31, 2)):

        @pl.when(gy == edge)
        def _():
            for p in range(3):
                r = 3 * p + q
                pool[4 * r : 4 * r + 4] = jnp.zeros((4, BLOCK, C), BF16)

    def chosen(k, f):
        return jnp.clip(map_ref[k, f], 0, 36)

    def weight_group(g):
        for j in range(PER_GROUP):
            k = g * PER_GROUP + j
            total = None
            for s in range(SLOTS // 2):
                pair = jnp.concatenate([pool[chosen(k, 2 * s)], pool[chosen(k, 2 * s + 1)]], axis=0)
                part = dot(fine_t[:, s * C : (s + 1) * C], pair)
                total = part if total is None else total + part
            total = total * (1.0 / math.sqrt(262144))
            acc[0, pl.ds(pl.multiple_of(k * C, C), C), :] = total[:, :HALF]
            acc[1, pl.ds(pl.multiple_of(k * C, C), C), :] = total[:, HALF:]

    def mate_copy(g):
        rows = pl.ds(pl.multiple_of(g * PER_GROUP * C, PER_GROUP * C), PER_GROUP * C)
        return remote(acc.at[1 - c, rows], from_mate.at[rows], m_send.at[g], m_recv.at[g], mate)

    first_at = jnp.where(c == 0, gx, z)
    second_at = jnp.where(c == 0, z, gx)

    def first_peer(a):
        return at(jnp.where(c == 0, a, gx), jnp.where(c == 0, z, a), y, c)

    def second_peer(b):
        return at(jnp.where(c == 0, gx, b), jnp.where(c == 0, b, z), y, c)

    def first_copy(a, b):
        slot = (first_at - a + 4) % 4 - 1
        return remote(send1.at[a, b], recv1.at[slot, b], s1_send.at[a, b], s1_recv.at[slot, b], first_peer(a))

    def ab(n):
        return jnp.where(c == 0, n // 4, n % 4), jnp.where(c == 0, n % 4, n // 4)

    def send_piece(n, carry):
        a, b = ab(n)
        rows = pl.ds(pl.multiple_of(n * PIECE, 16), PIECE)
        summed = acc[c, rows, :] + from_mate[rows, :]

        @pl.when(a == first_at)
        def _():
            total1[b] = summed

        @pl.when(a != first_at)
        def _():
            codes, scale = encode(summed)
            send1[a, b, 0:PIECE, :] = codes
            send1[a, b, PIECE:LONG, :] = scale
            first_copy(a, b).start()

        return carry

    def weight_step(g, carry):
        weight_group(g)
        mate_copy(g).start()
        return carry

    bounds = (0, 5, 10, 16)

    def send_group(g):
        mate_copy(g).wait_recv()
        lax.fori_loop(bounds[g], bounds[g + 1], send_piece, 0)

    weight_step(0, 0)
    weight_step(1, 0)
    send_group(0)
    weight_step(2, 0)
    send_group(1)
    send_group(2)

    def fine_part(s, width):
        rows = []
        for f in range(width):
            rows.append(jnp.concatenate([pool[chosen(k, s * width + f)] for k in range(K)], axis=1))
        got = dot(jnp.concatenate(rows, axis=0), weight_t[...]).astype(BF16)
        for f in range(width):
            slot = s * width + f
            fine_vmem[slot] = jnp.where(
                slot < count, got[f * BLOCK : (f + 1) * BLOCK], jnp.zeros((), BF16)
            )

    def fine_copy(s, width):
        return pltpu.make_async_copy(
            fine_vmem.at[pl.ds(s * width, width)], fine_out.at[pl.ds(s * width, width)], out_sem.at[s]
        )

    fine_part(0, 8)
    fine_copy(0, 8).start()

    def second_copy(b):
        slot = (second_at - b + 4) % 4 - 1
        return remote(send2.at[b], recv2.at[slot], s2_send.at[b], s2_recv.at[slot], second_peer(b))

    def second_step(b, carry):
        for slot in range(3):
            remote(recv1.at[slot, b], recv1.at[slot, b], s1_send.at[0, 0], s1_recv.at[slot, b], mate).wait_recv()
        summed = total1[b]
        for slot in range(3):
            summed = summed + decode(recv1.at[slot, b], PIECE)

        @pl.when(b == second_at)
        def _():
            total2[...] = summed

        @pl.when(b != second_at)
        def _():
            codes, scale = encode(summed)
            send2[b, 0:PIECE, :] = codes
            send2[b, PIECE:LONG, :] = scale
            second_copy(b).start()

        return carry

    lax.fori_loop(0, 4, second_step, 0)

    fine_part(1, 8)
    fine_copy(1, 8).start()

    starts = (0, 96, 208, 304)
    start = jnp.where(y == 0, 0, jnp.where(y == 1, 96, jnp.where(y == 2, 208, 304)))
    offset = y * 108 - start
    for slot in range(3):
        remote(recv2.at[slot], recv2.at[slot], s2_send.at[0], s2_recv.at[slot], mate).wait_recv()
    summed = total2[...]
    for slot in range(3):
        summed = summed + decode(recv2.at[slot], PIECE)
    total2[...] = summed

    def third_copy(t):
        slot = (y - t + 4) % 4 - 1
        return remote(send3.at[t], recv3.at[slot], s3_send.at[t], s3_recv.at[slot], at(gx, z, t, c))

    for t in range(4):

        @pl.when(y != t)
        def _():
            codes, scale = encode(total2[starts[t] : starts[t] + YROWS, :])
            send3[t, 0:YROWS, :] = codes
            send3[t, YROWS:YLONG, :] = scale
            third_copy(t).start()

    summed = total2[pl.ds(pl.multiple_of(start, 16), YROWS), :]
    for slot in range(3):
        remote(recv3.at[slot], recv3.at[slot], s3_send.at[0], s3_recv.at[slot], mate).wait_recv()
        summed = summed + decode(recv3.at[slot], YROWS)
    total3[...] = summed

    own_rows[0:MINE, :] = total3[pl.ds(offset + MINE * (1 - c), MINE), :]
    last = remote(own_rows, mate_rows, f_sem.at[0], f_sem.at[1], mate)
    last.start()
    weight_vmem[:, pl.ds(pl.multiple_of(c * HALF, HALF), HALF)] = total3[pl.ds(offset + MINE * c, MINE), :]
    last.wait_recv()
    weight_vmem[:, pl.ds(pl.multiple_of((1 - c) * HALF, HALF), HALF)] = mate_rows[0:MINE, :]
    final = pltpu.make_async_copy(weight_vmem, weight_out, out_sem.at[2])
    final.start()

    for g in range(GROUPS):
        mate_copy(g).wait_send()

    def drain(n, carry):
        a, b = ab(n)

        @pl.when(a != first_at)
        def _():
            first_copy(a, b).wait_send()

        return carry

    lax.fori_loop(0, PIECES, drain, 0)
    for t in range(4):

        @pl.when(second_at != t)
        def _():
            second_copy(t).wait_send()

        @pl.when(y != t)
        def _():
            third_copy(t).wait_send()

    last.wait_send()
    fine_copy(0, 8).wait()
    fine_copy(1, 8).wait()
    final.wait()


def local(fine_feat, coarse_grad, kernel_map, counts, weight):
    anywhere = pl.BlockSpec(memory_space=pl.ANY)
    smem = pl.BlockSpec(memory_space=pltpu.SMEM)
    dma = pltpu.SemaphoreType.DMA
    fine, weight_grad = pl.pallas_call(
        kernel,
        out_shape=(
            jax.ShapeDtypeStruct((SLOTS, BLOCK, C), BF16),
            jax.ShapeDtypeStruct((MINE, C), F32),
        ),
        in_specs=[anywhere, anywhere, smem, smem, anywhere],
        out_specs=(anywhere, anywhere),
        scratch_shapes=[
            pltpu.VMEM((37, BLOCK, C), BF16),
            pltpu.VMEM((SLOTS, BLOCK, C), BF16),
            pltpu.VMEM((C, SLOTS * BLOCK), BF16),
            pltpu.VMEM((K, C, C), BF16),
            pltpu.VMEM((K * C, C), BF16),
            pltpu.VMEM((2, K * C, HALF), F32),
            pltpu.VMEM((K * C, HALF), F32),
            pltpu.VMEM((4, 4, LONG, HALF), I16),
            pltpu.VMEM((3, 4, LONG, HALF), I16),
            pltpu.VMEM((4, PIECE, HALF), F32),
            pltpu.VMEM((4, LONG, HALF), I16),
            pltpu.VMEM((3, LONG, HALF), I16),
            pltpu.VMEM((PIECE, HALF), F32),
            pltpu.VMEM((4, YLONG, HALF), I16),
            pltpu.VMEM((3, YLONG, HALF), I16),
            pltpu.VMEM((YROWS, HALF), F32),
            pltpu.VMEM((56, HALF), F32),
            pltpu.VMEM((56, HALF), F32),
            pltpu.VMEM((SLOTS, BLOCK, C), BF16),
            pltpu.VMEM((MINE, C), F32),
            dma((3,)), dma((2,)), dma((2,)), dma((2, 3)), dma((2, 3)), dma((GROUPS,)), dma((GROUPS,)),
            dma((4, 4)), dma((3, 4)), dma((4,)), dma((3,)), dma((4,)), dma((3,)), dma((2,)),
            dma((3,)),
        ],
        compiler_params=pltpu.CompilerParams(
            collective_id=0, has_side_effects=True, vmem_limit_bytes=56 << 20
        ),
        cost_estimate=pl.CostEstimate(flops=14_500_000_000, bytes_accessed=8_000_000, transcendentals=0),
    )(fine_feat[0, 0], coarse_grad[0, 0], kernel_map[0, 0], counts, weight)
    return fine[None, None], weight_grad


def solution(mesh):
    return jax.shard_map(
        local,
        mesh=mesh,
        in_specs=(
            P("gx", "gy", None, None, None),
            P("gx", "gy", None, None, None),
            P("gx", "gy", None, None),
            P("gx", "gy"),
            P(),
        ),
        out_specs=(P("gx", "gy", None, None, None), P(("gx", "gy"), None)),
        check_vma=False,
    )
```

```python
import functools
import math

import jax
import jax.numpy as jnp
from jax import lax
from jax.experimental import pallas as pl
from jax.experimental.pallas import tpu as pltpu
from jax.sharding import PartitionSpec as P

MESH = pl.DeviceIdType.MESH
F32, BF16, I16 = jnp.float32, jnp.bfloat16, jnp.int16
K, C, BLOCK, SLOTS, COARSE = 27, 256, 128, 16, 4
HALF = C // 2
GROUPS, PER_GROUP = 4, 7
UNIT = 108
LONG = 112
MINE = 54
LEVELS = 32767.0

dot = functools.partial(jnp.dot, preferred_element_type=F32)


def encode(values):
    held = lax.broadcasted_iota(jnp.int32, (LONG, HALF), 0) < UNIT
    top = jnp.max(jnp.where(held, jnp.abs(values), 0.0), axis=0, keepdims=True)
    power = jnp.ceil(jnp.log2(jnp.maximum(top, 1e-35)) + 1e-3)
    codes = jnp.floor(values * (jnp.exp2(-power) * LEVELS) + 0.5)
    return jnp.where(held, codes, power).astype(jnp.int32).astype(I16)


def decode(unit):
    codes = unit.astype(jnp.int32).astype(F32)
    return codes * (jnp.exp2(codes[UNIT : UNIT + 1, :]) * (1.0 / LEVELS))


def kernel(
    fine_hbm, coarse_hbm, map_ref, counts_ref, weight_hbm,
    fine_out, weight_out,
    pool, fine_in, fine_t, weight_in, weight_t, acc, from_mate,
    send1, recv1, send2, recv2, total2, total3,
    own_rows, mate_rows, fine_vmem, weight_vmem,
    load_sem, hx_send, hx_recv, hy_send, hy_recv, m_send, m_recv,
    s1_send, s1_recv, s2_send, s2_recv, f_sem, out_sem,
):
    gx, gy = lax.axis_index("gx"), lax.axis_index("gy")
    z, y, c = gy // 8, (gy // 2) % 4, gy % 2

    def at(x_, z_, y_, c_):
        return (x_, z_ * 8 + y_ * 2 + c_)

    mate = at(gx, z, y, 1 - c)
    up, down = (gx, (gy + 1) % 32), (gx, (gy + 31) % 32)
    away = (gx, (gy + jnp.where(c == 0, 31, 1)) % 32)

    loads = [
        pltpu.make_async_copy(coarse_hbm, pool.at[16:20], load_sem.at[0]),
        pltpu.make_async_copy(fine_hbm, fine_in, load_sem.at[1]),
        pltpu.make_async_copy(weight_hbm, weight_in, load_sem.at[2]),
    ]
    for copy in loads:
        copy.start()

    barrier = pltpu.get_barrier_semaphore()
    first_at = jnp.where(c == 0, z, y)
    third_at = jnp.where(c == 0, y, z)

    def first_peer(a):
        return at(gx, jnp.where(c == 0, a, z), jnp.where(c == 0, y, a), c)

    def plane_peer(b, d):
        return at(b, jnp.where(c == 0, z, d), jnp.where(c == 0, d, y), c)

    partners = [mate, away] + [first_peer((first_at + s) % 4) for s in (1, 2, 3)]
    partners += [plane_peer((gx + e // 4) % 4, (third_at + e % 4) % 4) for e in range(1, 16)]
    for who in partners:
        pl.semaphore_signal(barrier, inc=1, device_id=who, device_id_type=MESH)
    pl.semaphore_wait(barrier, len(partners))

    def remote(src, dst, send, recv, who):
        return pltpu.make_async_remote_copy(
            src_ref=src, dst_ref=dst, send_sem=send, recv_sem=recv, device_id=who, device_id_type=MESH
        )

    def region(r):
        return pool.at[4 * r : 4 * r + 4]

    halo = []

    def along_x(j):
        for i, (who, r) in enumerate(((((gx + 1) % 4, gy), 1), (((gx + 3) % 4, gy), 7))):
            copy = remote(coarse_hbm.at[j], pool.at[4 * r + j], hx_send.at[i, j], hx_recv.at[i, j], who)
            copy.start()
            halo.append((copy, i, j))

    halo_y = []

    def along_y(p, j, src):
        for i, (who, q) in enumerate(((up, 0), (down, 2))):
            at_block = 4 * (3 * p + q) + j
            copy = remote(src, pool.at[at_block], hy_send.at[i, p, j], hy_recv.at[i, p, j], who)
            copy.start()
            halo_y.append(copy)

    for j in range(COARSE):
        along_x(j)
        along_y(1, j, coarse_hbm.at[j])

    pool[36] = jnp.zeros((BLOCK, C), BF16)
    count = counts_ref[0, 0]
    loads[1].wait()
    for f in range(SLOTS):
        block = jnp.where(f < count, fine_in[f], jnp.zeros((), BF16))
        fine_t[:, f * BLOCK : (f + 1) * BLOCK] = block.T

    for copy, i, j in halo:
        copy.wait_recv()
        along_y(2 * i, j, pool.at[4 * (1 + 6 * i) + j])
    loads[2].wait()

    def turn(k, carry):
        weight_t[pl.ds(pl.multiple_of(k * C, C), C), :] = weight_in[k].T
        return carry

    lax.fori_loop(0, K, turn, 0)
    loads[0].wait()
    for copy, _, _ in halo:
        copy.wait_send()
    for copy in halo_y:
        copy.wait()

    @pl.when(gx == 0)
    def _():
        pool[0:12] = jnp.zeros((12, BLOCK, C), BF16)

    @pl.when(gx == 3)
    def _():
        pool[24:36] = jnp.zeros((12, BLOCK, C), BF16)

    for edge, q in ((0, 0), (31, 2)):

        @pl.when(gy == edge)
        def _():
            for p in range(3):
                r = 3 * p + q
                pool[4 * r : 4 * r + 4] = jnp.zeros((4, BLOCK, C), BF16)

    def chosen(k, f):
        return jnp.clip(map_ref[k, f], 0, 36)

    acc[:, K * C : K * C + 8, :] = jnp.zeros((2, 8, HALF), F32)
    from_mate[K * C : K * C + 8, :] = jnp.zeros((8, HALF), F32)

    def weight_group(g):
        for k in range(g * PER_GROUP, min(K, (g + 1) * PER_GROUP)):
            total = None
            for s in range(SLOTS // 2):
                pair = jnp.concatenate([pool[chosen(k, 2 * s)], pool[chosen(k, 2 * s + 1)]], axis=0)
                part = dot(fine_t[:, s * C : (s + 1) * C], pair)
                total = part if total is None else total + part
            total = total * (1.0 / math.sqrt(262144))
            acc[0, k * C : (k + 1) * C, :] = total[:, :HALF]
            acc[1, k * C : (k + 1) * C, :] = total[:, HALF:]
        mate_copy(g).start()

    def mate_copy(g):
        rows = pl.ds(g * PER_GROUP * C, (min(K, (g + 1) * PER_GROUP) - g * PER_GROUP) * C)
        return remote(acc.at[1 - c, rows], from_mate.at[rows], m_send.at[g], m_recv.at[g], mate)

    def summed_unit(b, a, d):
        start = UNIT * (16 * b + jnp.where(c == 0, 4 * a + d, 4 * d + a))
        return acc[c, pl.ds(start, LONG), :] + from_mate[pl.ds(start, LONG), :]

    def first_copy(a, b):
        slot = (first_at - a + 4) % 4 - 1
        return remote(send1.at[a, b], recv1.at[slot, b], s1_send.at[a, b], s1_recv.at[slot, b], first_peer(a))

    def first_stage(b):
        mate_copy(b).wait_recv()

        def step(s, carry):
            a = (first_at + s) % 4
            for d in range(4):
                send1[a, b, d] = encode(summed_unit(b, a, d))
            first_copy(a, b).start()
            return carry

        lax.fori_loop(1, 4, step, 0)

    def second_copy(b, d):
        e = 4 * ((gx - b + 4) % 4) + (third_at - d + 4) % 4 - 1
        return remote(send2.at[b, d], recv2.at[e], s2_send.at[b, d], s2_recv.at[e], plane_peer(b, d))

    def second_stage(b):
        for slot in range(3):
            remote(recv1.at[slot, b], recv1.at[slot, b], s1_send.at[0, 0], s1_recv.at[slot, b], mate).wait_recv()

        def step(d, carry):
            summed = summed_unit(b, first_at, d)
            for slot in range(3):
                summed = summed + decode(recv1[slot, b, d])
            here = (b == gx) & (d == third_at)

            @pl.when(here)
            def _():
                total2[...] = summed

            @pl.when(jnp.logical_not(here))
            def _():
                send2[b, d] = encode(summed)
                second_copy(b, d).start()

            return carry

        lax.fori_loop(0, 4, step, 0)

    def fine_part(s, width):
        rows = []
        for f in range(width):
            rows.append(jnp.concatenate([pool[chosen(k, s * width + f)] for k in range(K)], axis=1))
        got = dot(jnp.concatenate(rows, axis=0), weight_t[...]).astype(BF16)
        for f in range(width):
            slot = s * width + f
            fine_vmem[slot] = jnp.where(
                slot < count, got[f * BLOCK : (f + 1) * BLOCK], jnp.zeros((), BF16)
            )

    def fine_copy(s, width):
        return pltpu.make_async_copy(
            fine_vmem.at[pl.ds(s * width, width)], fine_out.at[pl.ds(s * width, width)], out_sem.at[s]
        )

    def fine_step(s):
        fine_part(s, 4)
        fine_copy(s, 4).start()


    weight_group(0)
    weight_group(1)
    first_stage(0)
    weight_group(2)
    first_stage(1)
    weight_group(3)
    first_stage(2)
    second_stage(0)
    first_stage(3)
    second_stage(1)
    fine_step(0)
    second_stage(2)
    fine_step(1)
    second_stage(3)
    fine_step(2)
    fine_step(3)

    def last_step(e, summed):
        remote(recv2.at[e], recv2.at[e], s2_send.at[0, 0], s2_recv.at[e], mate).wait_recv()
        return summed + decode(recv2[e])

    total3[...] = lax.fori_loop(0, 15, last_step, total2[...])

    own_rows[0:MINE, :] = total3[pl.ds(MINE * (1 - c), MINE), :]
    last = remote(own_rows, mate_rows, f_sem.at[0], f_sem.at[1], mate)
    last.start()
    weight_vmem[:, pl.ds(pl.multiple_of(c * HALF, HALF), HALF)] = total3[pl.ds(MINE * c, MINE), :]
    last.wait_recv()
    weight_vmem[:, pl.ds(pl.multiple_of((1 - c) * HALF, HALF), HALF)] = mate_rows[0:MINE, :]
    final = pltpu.make_async_copy(weight_vmem, weight_out, out_sem.at[4])
    final.start()

    for g in range(GROUPS):
        mate_copy(g).wait_send()

    def drain_first(n, carry):
        first_copy((first_at + 1 + n // 4) % 4, n % 4).wait_send()
        return carry

    lax.fori_loop(0, 12, drain_first, 0)

    def drain_second(e, carry):
        second_copy((gx + e // 4) % 4, (third_at + e % 4) % 4).wait_send()
        return carry

    lax.fori_loop(1, 16, drain_second, 0)
    last.wait_send()
    for s in range(4):
        fine_copy(s, 4).wait()
    final.wait()


def local(fine_feat, coarse_grad, kernel_map, counts, weight):
    anywhere = pl.BlockSpec(memory_space=pl.ANY)
    smem = pl.BlockSpec(memory_space=pltpu.SMEM)
    dma = pltpu.SemaphoreType.DMA
    fine, weight_grad = pl.pallas_call(
        kernel,
        out_shape=(
            jax.ShapeDtypeStruct((SLOTS, BLOCK, C), BF16),
            jax.ShapeDtypeStruct((MINE, C), F32),
        ),
        in_specs=[anywhere, anywhere, smem, smem, anywhere],
        out_specs=(anywhere, anywhere),
        scratch_shapes=[
            pltpu.VMEM((37, BLOCK, C), BF16),
            pltpu.VMEM((SLOTS, BLOCK, C), BF16),
            pltpu.VMEM((C, SLOTS * BLOCK), BF16),
            pltpu.VMEM((K, C, C), BF16),
            pltpu.VMEM((K * C, C), BF16),
            pltpu.VMEM((2, K * C + 8, HALF), F32),
            pltpu.VMEM((K * C + 8, HALF), F32),
            pltpu.VMEM((4, 4, 4, LONG, HALF), I16),
            pltpu.VMEM((3, 4, 4, LONG, HALF), I16),
            pltpu.VMEM((4, 4, LONG, HALF), I16),
            pltpu.VMEM((15, LONG, HALF), I16),
            pltpu.VMEM((LONG, HALF), F32),
            pltpu.VMEM((LONG, HALF), F32),
            pltpu.VMEM((56, HALF), F32),
            pltpu.VMEM((56, HALF), F32),
            pltpu.VMEM((SLOTS, BLOCK, C), BF16),
            pltpu.VMEM((MINE, C), F32),
            dma((3,)), dma((2, 4)), dma((2, 4)), dma((2, 3, 4)), dma((2, 3, 4)), dma((GROUPS,)), dma((GROUPS,)),
            dma((4, 4)), dma((3, 4)), dma((4, 4)), dma((15,)), dma((2,)), dma((5,)),
        ],
        compiler_params=pltpu.CompilerParams(
            collective_id=0, has_side_effects=True, vmem_limit_bytes=56 << 20
        ),
        cost_estimate=pl.CostEstimate(flops=14_500_000_000, bytes_accessed=8_000_000, transcendentals=0),
    )(fine_feat[0, 0], coarse_grad[0, 0], kernel_map[0, 0], counts, weight)
    return fine[None, None], weight_grad


def solution(mesh):
    return jax.shard_map(
        local,
        mesh=mesh,
        in_specs=(
            P("gx", "gy", None, None, None),
            P("gx", "gy", None, None, None),
            P("gx", "gy", None, None),
            P("gx", "gy"),
            P(),
        ),
        out_specs=(P("gx", "gy", None, None, None), P(("gx", "gy"), None)),
        check_vma=False,
    )
```

```python
import functools
import math

import jax
import jax.numpy as jnp
from jax import lax
from jax.experimental import pallas as pl
from jax.experimental.pallas import tpu as pltpu
from jax.sharding import PartitionSpec as P

MESH = pl.DeviceIdType.MESH
F32, BF16, I16 = jnp.float32, jnp.bfloat16, jnp.int16
K, C, BLOCK, SLOTS, COARSE = 27, 256, 128, 16, 4
HALF = C // 2
ENDS = (8, 15, 21, 27)
UNIT = 108
LONG = 112
MINE = 54
ROWS = 64
LEVELS = 32767.0

dot = functools.partial(jnp.dot, preferred_element_type=F32)


def encode(values):
    held = lax.broadcasted_iota(jnp.int32, (LONG, HALF), 0) < UNIT
    top = jnp.max(jnp.where(held, jnp.abs(values), 0.0), axis=0, keepdims=True)
    power = jnp.ceil(jnp.log2(jnp.maximum(top, 1e-35)) + 1e-3)
    codes = jnp.floor(values * (jnp.exp2(-power) * LEVELS) + 0.5)
    return jnp.where(held, codes, power).astype(jnp.int32).astype(I16)


def decode(unit):
    codes = unit.astype(jnp.int32).astype(F32)
    return codes * (jnp.exp2(codes[UNIT : UNIT + 1, :]) * (1.0 / LEVELS))


def kernel(
    fine_hbm, coarse_hbm, map_ref, counts_ref, weight_hbm,
    fine_out, weight_out,
    pool_low, pool_high, fine_in, fine_t, weight_in, weight_t, acc, from_mate,
    send1, recv1, send2, recv2, send3, recv3, total2, total3,
    own_rows, mate_rows,
    load_sem, hx_send, hx_recv, hy_send, hy_recv, m_send, m_recv,
    s1_send, s1_recv, s2_send, s2_recv, s3_send, s3_recv, f_sem,
):
    pools = (pool_low, pool_high)
    gx, gy = lax.axis_index("gx"), lax.axis_index("gy")
    z, y, c = gy // 8, (gy // 2) % 4, gy % 2

    def at(x_, z_, y_, c_):
        return (x_, z_ * 8 + y_ * 2 + c_)

    mate = at(gx, z, y, 1 - c)
    up, down = (gx, (gy + 1) % 32), (gx, (gy + 31) % 32)
    away = (gx, (gy + jnp.where(c == 0, 31, 1)) % 32)

    loads = [
        pltpu.make_async_copy(coarse_hbm.at[:, 0:ROWS], pool_low.at[16:20], load_sem.at[0]),
        pltpu.make_async_copy(fine_hbm, fine_in, load_sem.at[1]),
        pltpu.make_async_copy(weight_hbm, weight_in, load_sem.at[2]),
        pltpu.make_async_copy(coarse_hbm.at[:, ROWS:BLOCK], pool_high.at[16:20], load_sem.at[3]),
    ]
    for copy in loads:
        copy.start()

    barrier = pltpu.get_barrier_semaphore()
    first_at = jnp.where(c == 0, z, y)
    third_at = jnp.where(c == 0, y, z)

    def first_peer(a):
        return at(gx, jnp.where(c == 0, a, z), jnp.where(c == 0, y, a), c)

    def third_peer(d):
        return at(gx, jnp.where(c == 0, z, d), jnp.where(c == 0, d, y), c)

    partners = [mate, away]
    for s in (1, 2, 3):
        partners += [first_peer((first_at + s) % 4), ((gx + s) % 4, gy), third_peer((third_at + s) % 4)]
    for who in partners:
        pl.semaphore_signal(barrier, inc=1, device_id=who, device_id_type=MESH)
    pl.semaphore_wait(barrier, len(partners))

    def remote(src, dst, send, recv, who):
        return pltpu.make_async_remote_copy(
            src_ref=src, dst_ref=dst, send_sem=send, recv_sem=recv, device_id=who, device_id_type=MESH
        )

    ORDER = [(h, j) for h in range(2) for j in range(2)]

    def own(h, j):
        return coarse_hbm.at[pl.ds(2 * j, 2), pl.ds(ROWS * h, ROWS)]

    def part(r, h, j):
        return pools[h].at[pl.ds(4 * r + 2 * j, 2)]

    def x_copy(i, h, j):
        who, r = (((gx + 1) % 4, gy), 1) if i == 0 else (((gx + 3) % 4, gy), 7)
        return remote(own(h, j), part(r, h, j), hx_send.at[i, h, j], hx_recv.at[i, h, j], who)

    def y_copy(i, p, h, j):
        who = (gx, (gy + jnp.where(i == 0, 1, 31)) % 32)
        src = own(h, j) if p == 1 else part(3 * p + 1, h, j)
        return remote(src, part(3 * p + 2 * i, h, j), hy_send.at[i, p, h, j], hy_recv.at[i, p, h, j], who)

    def corner_copy(p):
        who = ((gx + 1 + p) % 4, gy)
        src, dst = part(3 + 2 * c, 1, 1), part(3 * p + 2 * c, 1, 1)
        return remote(src, dst, hy_send.at[1 - c, p, 1, 1], hy_recv.at[c, p, 1, 1], who)

    def own_along_y(h, j):
        for i in range(2):
            y_copy(i, 1, h, j).start()

    for h, j in ORDER:
        for i in range(2):
            x_copy(i, h, j).start()
    own_along_y(0, 0)
    own_along_y(0, 1)
    own_along_y(1, 1)

    def forward(h, j):
        for p in (0, 2):
            x_copy(p // 2, h, j).wait_recv()
            if (h, j) == (1, 1):
                y_copy(c, p, h, j).start()
            else:
                for i in range(2):
                    y_copy(i, p, h, j).start()

    def halo_done(h):
        for j in range(2):
            for i in range(2):
                for p in range(3):
                    if (p, h, j) != (1, 1, 1):
                        y_copy(i, p, h, j).wait_recv()
                for p in (0, 2):
                    y_copy(i, p, h, j).wait_send()

        @pl.when(gx == 0)
        def _():
            pools[h][0:12] = jnp.zeros((12, ROWS, C), BF16)

        @pl.when(gx == 3)
        def _():
            pools[h][24:36] = jnp.zeros((12, ROWS, C), BF16)

        for edge, q in ((0, 0), (31, 2)):

            @pl.when(gy == edge)
            def _():
                for p in range(3):
                    r = 3 * p + q
                    pools[h][4 * r : 4 * r + 4] = jnp.zeros((4, ROWS, C), BF16)

    for pool in pools:
        pool[36] = jnp.zeros((ROWS, C), BF16)
    count = counts_ref[0, 0]
    loads[1].wait()
    for f in range(SLOTS // 4):
        blocks = [jnp.where(4 * f + i < count, fine_in[4 * f + i], jnp.zeros((), BF16)) for i in range(4)]
        for h in range(2):
            quad = jnp.concatenate([block[ROWS * h : ROWS * (h + 1)] for block in blocks], axis=0)
            fine_t[h, :, f * C : (f + 1) * C] = quad.T
    acc[:, K * C : K * C + 8, :] = jnp.zeros((2, 8, HALF), F32)
    from_mate[K * C : K * C + 8, :] = jnp.zeros((8, HALF), F32)
    loads[0].wait()
    loads[3].wait()
    loads[2].wait()

    def turn(k, carry):
        weight_t[pl.ds(pl.multiple_of(k * C, C), C), :] = weight_in[k].T
        return carry

    forward(0, 0)
    lax.fori_loop(0, 9, turn, 0)
    forward(0, 1)
    own_along_y(1, 0)
    for i in range(2):
        y_copy(i, 1, 1, 1).wait_recv()
    for p in (0, 2):
        corner_copy(p).start()
    lax.fori_loop(9, 18, turn, 0)
    forward(1, 0)
    lax.fori_loop(18, K, turn, 0)
    forward(1, 1)
    halo_done(0)

    def chosen(k, f):
        return jnp.clip(map_ref[f, k], 0, 36)

    def weight_offset(k, h):
        total = None
        for s in range(SLOTS // 4):
            quad = [pools[h][chosen(k, 4 * s + i)] for i in range(4)]
            piece = dot(fine_t[h, :, s * C : (s + 1) * C], jnp.concatenate(quad, axis=0))
            total = piece if total is None else total + piece
        return total * (1.0 / math.sqrt(262144))

    def first_half(g, carry):
        for i in range(9):
            k = 9 * g + i
            total = weight_offset(k, 0)
            for side in range(2):
                acc[side, pl.ds(pl.multiple_of(k * C, C), C), :] = total[:, side * HALF : (side + 1) * HALF]
        return carry

    begin = (gx + 1) % 4
    begin = jnp.where(begin == 0, 0, jnp.where(begin == 1, 6, jnp.where(begin == 2, 13, 20)))

    def rows_of(n):
        return pl.ds(pl.multiple_of((begin + n) % K * C, C), C)

    def mate_copy(n):
        rows = rows_of(n)
        return remote(acc.at[1 - c, rows], from_mate.at[rows], m_send.at[n], m_recv.at[n], mate)

    def members(g):
        return range(0 if g == 0 else ENDS[g - 1], ENDS[g])

    def weight_group(start, end):
        for n in range(start, end):
            total = weight_offset((begin + n) % K, 1)
            for side in range(2):
                acc[side, rows_of(n), :] += total[:, side * HALF : (side + 1) * HALF]
        for n in range(start, end):
            mate_copy(n).start()

    def summed_unit(g, a, d):
        start = UNIT * (16 * ((gx + 1 + g) % 4) + jnp.where(c == 0, 4 * a + d, 4 * d + a))
        return acc[c, pl.ds(start, LONG), :] + from_mate[pl.ds(start, LONG), :]

    def first_copy(g, s):
        who = first_peer((first_at + s) % 4)
        return remote(send1.at[s - 1, g], recv1.at[3 - s, g], s1_send.at[s - 1, g], s1_recv.at[3 - s, g], who)

    def first_stage(g):
        for n in members(g):
            mate_copy(n).wait_recv()
        for s in (2, 1, 3):
            for d in range(4):
                send1[s - 1, g, d] = encode(summed_unit(g, (first_at + s) % 4, d))
            first_copy(g, s).start()

    def second_copy(g):
        return remote(send2.at[g], recv2.at[g], s2_send.at[g], s2_recv.at[g], ((gx + 1 + g) % 4, gy))

    def third_copy(d):
        slot = (third_at - d + 4) % 4 - 1
        return remote(send3.at[d], recv3.at[slot], s3_send.at[d], s3_recv.at[slot], third_peer(d))

    def second_stage(g):
        for s in (1, 2, 3):
            first_copy(g, s).wait_recv()
        if g == 3:
            for slot in range(3):
                second_copy(slot).wait_recv()
        for d in range(4):
            summed = summed_unit(g, first_at, d)
            for slot in range(3):
                summed = summed + decode(recv1[slot, g, d])
            if g < 3:
                send2[g, d] = encode(summed)
                continue
            for slot in range(3):
                summed = summed + decode(recv2[slot, d])

            @pl.when(d == third_at)
            def _():
                total2[...] = summed

            @pl.when(d != third_at)
            def _():
                send3[d] = encode(summed)
                third_copy(d).start()

        if g < 3:
            second_copy(g).start()

    def fine_part(s, width):
        rows = []
        for f in range(width):
            for pool in pools:
                rows.append(jnp.concatenate([pool[chosen(k, s * width + f)] for k in range(K)], axis=1))
        got = dot(jnp.concatenate(rows, axis=0), weight_t[...]).astype(BF16)
        for f in range(width):
            slot = s * width + f
            fine_out[slot] = jnp.where(
                slot < count, got[f * BLOCK : (f + 1) * BLOCK], jnp.zeros((), BF16)
            )

    def fine_step(s):
        fine_part(s, 2)


    lax.fori_loop(0, 3, first_half, 0)
    halo_done(1)
    weight_group(0, 4)
    weight_group(4, 8)
    weight_group(8, 15)
    first_stage(0)
    weight_group(15, 21)
    first_stage(1)
    weight_group(21, 27)
    first_stage(2)
    fine_step(0)
    first_stage(3)
    second_stage(0)
    fine_step(1)
    fine_step(2)
    second_stage(1)
    fine_step(3)
    fine_step(4)
    second_stage(2)
    fine_step(5)
    fine_step(6)
    second_stage(3)
    fine_step(7)

    summed = total2[...]
    for e in range(3):
        remote(recv3.at[e], recv3.at[e], s3_send.at[0], s3_recv.at[e], mate).wait_recv()
        summed = summed + decode(recv3[e])
    total3[...] = summed

    own_rows[0:MINE, :] = total3[pl.ds(MINE * (1 - c), MINE), :]
    last = remote(own_rows, mate_rows, f_sem.at[0], f_sem.at[1], mate)
    last.start()
    weight_out[:, pl.ds(pl.multiple_of(c * HALF, HALF), HALF)] = total3[pl.ds(MINE * c, MINE), :]
    last.wait_recv()
    weight_out[:, pl.ds(pl.multiple_of((1 - c) * HALF, HALF), HALF)] = mate_rows[0:MINE, :]

    for h, j in ORDER:
        for i in range(2):
            x_copy(i, h, j).wait_send()
            y_copy(i, 1, h, j).wait_send()

    def drain_mate(n, carry):
        mate_copy(n).wait_send()
        return carry

    lax.fori_loop(0, K, drain_mate, 0)
    for g in range(4):
        for s in (1, 2, 3):
            first_copy(g, s).wait_send()
        if g < 3:
            second_copy(g).wait_send()

        @pl.when(g != third_at)
        def _():
            third_copy(g).wait_send()

    last.wait_send()


def finish(fine_in, weight_in, fine_out, weight_out, sems):
    copies = [pltpu.make_async_copy(weight_in, weight_out, sems.at[4])]
    for s in range(4):
        rows = pl.ds(4 * s, 4)
        copies.append(pltpu.make_async_copy(fine_in.at[rows], fine_out.at[rows], sems.at[s]))
    for copy in copies:
        copy.start()
    for copy in copies:
        copy.wait()


def local(fine_feat, coarse_grad, kernel_map, counts, weight):
    anywhere = pl.BlockSpec(memory_space=pl.ANY)
    smem = pl.BlockSpec(memory_space=pltpu.SMEM)
    vmem = pl.BlockSpec(memory_space=pltpu.VMEM)
    dma = pltpu.SemaphoreType.DMA
    fine, weight_grad = pl.pallas_call(
        kernel,
        out_shape=(pltpu.VMEM((SLOTS, BLOCK, C), BF16), pltpu.VMEM((MINE, C), F32)),
        in_specs=[anywhere, anywhere, smem, smem, anywhere],
        out_specs=(vmem, vmem),
        scratch_shapes=[
            pltpu.VMEM((37, ROWS, C), BF16),
            pltpu.VMEM((37, ROWS, C), BF16),
            pltpu.VMEM((SLOTS, BLOCK, C), BF16),
            pltpu.VMEM((2, C, SLOTS * ROWS), BF16),
            pltpu.VMEM((K, C, C), BF16),
            pltpu.VMEM((K * C, C), BF16),
            pltpu.VMEM((2, K * C + 8, HALF), F32),
            pltpu.VMEM((K * C + 8, HALF), F32),
            pltpu.VMEM((3, 4, 4, LONG, HALF), I16),
            pltpu.VMEM((3, 4, 4, LONG, HALF), I16),
            pltpu.VMEM((3, 4, LONG, HALF), I16),
            pltpu.VMEM((3, 4, LONG, HALF), I16),
            pltpu.VMEM((4, LONG, HALF), I16),
            pltpu.VMEM((3, LONG, HALF), I16),
            pltpu.VMEM((LONG, HALF), F32),
            pltpu.VMEM((LONG, HALF), F32),
            pltpu.VMEM((56, HALF), F32),
            pltpu.VMEM((56, HALF), F32),
            dma((4,)), dma((2, 2, 2)), dma((2, 2, 2)), dma((2, 3, 2, 2)), dma((2, 3, 2, 2)), dma((K,)), dma((K,)),
            dma((3, 4)), dma((3, 4)), dma((3,)), dma((3,)), dma((4,)), dma((3,)), dma((2,)),
        ],
        compiler_params=pltpu.CompilerParams(
            collective_id=0, has_side_effects=True, vmem_limit_bytes=56 << 20
        ),
        cost_estimate=pl.CostEstimate(flops=14_500_000_000, bytes_accessed=8_000_000, transcendentals=0),
    )(fine_feat[0, 0], coarse_grad[0, 0], kernel_map[0, 0].T, counts, weight)
    fine, weight_grad = pl.pallas_call(
        finish,
        out_shape=(
            jax.ShapeDtypeStruct((SLOTS, BLOCK, C), BF16),
            jax.ShapeDtypeStruct((MINE, C), F32),
        ),
        in_specs=[vmem, vmem],
        out_specs=(anywhere, anywhere),
        scratch_shapes=[dma((5,))],
        compiler_params=pltpu.CompilerParams(vmem_limit_bytes=8 << 20),
    )(fine, weight_grad)
    return fine[None, None], weight_grad


def solution(mesh):
    return jax.shard_map(
        local,
        mesh=mesh,
        in_specs=(
            P("gx", "gy", None, None, None),
            P("gx", "gy", None, None, None),
            P("gx", "gy", None, None),
            P("gx", "gy"),
            P(),
        ),
        out_specs=(P("gx", "gy", None, None, None), P(("gx", "gy"), None)),
        check_vma=False,
    )
```

```python
import functools
import math

import jax
import jax.numpy as jnp
from jax import lax
from jax.experimental import pallas as pl
from jax.experimental.pallas import tpu as pltpu
from jax.sharding import PartitionSpec as P

MESH = pl.DeviceIdType.MESH
F32, BF16, I16 = jnp.float32, jnp.bfloat16, jnp.int16
K, C, BLOCK, SLOTS, COARSE = 27, 256, 128, 16, 4
HALF = C // 2
ENDS = (8, 15, 21, 27)
UNIT = 108
LONG = 112
MINE = 54
ROWS = 64
LEVELS = 32767.0

dot = functools.partial(jnp.dot, preferred_element_type=F32)


def encode(values):
    held = lax.broadcasted_iota(jnp.int32, (LONG, HALF), 0) < UNIT
    top = jnp.max(jnp.where(held, jnp.abs(values), 0.0), axis=0, keepdims=True)
    power = jnp.ceil(jnp.log2(jnp.maximum(top, 1e-35)) + 1e-3)
    codes = jnp.floor(values * (jnp.exp2(-power) * LEVELS) + 0.5)
    return jnp.where(held, codes, power).astype(jnp.int32).astype(I16)


def decode(unit):
    codes = unit.astype(jnp.int32).astype(F32)
    return codes * (jnp.exp2(codes[UNIT : UNIT + 1, :]) * (1.0 / LEVELS))


def kernel(
    fine_hbm, coarse_hbm, map_ref, counts_ref, weight_hbm,
    fine_out, weight_out,
    pool_low, pool_high, fine_in, fine_t, weight_in, weight_t, acc, from_mate,
    send1, recv1, send2, recv2, send3, recv3, total2, total3,
    own_rows, mate_rows,
    load_sem, hx_send, hx_recv, hy_send, hy_recv, m_send, m_recv,
    s1_send, s1_recv, s2_send, s2_recv, s3_send, s3_recv, f_sem,
):
    pools = (pool_low, pool_high)
    gx, gy = lax.axis_index("gx"), lax.axis_index("gy")
    z, y, c = gy // 8, (gy // 2) % 4, gy % 2

    def at(x_, z_, y_, c_):
        return (x_, z_ * 8 + y_ * 2 + c_)

    mate = at(gx, z, y, 1 - c)
    up, down = (gx, (gy + 1) % 32), (gx, (gy + 31) % 32)
    away = (gx, (gy + jnp.where(c == 0, 31, 1)) % 32)

    loads = [
        pltpu.make_async_copy(coarse_hbm.at[:, 0:ROWS], pool_low.at[16:20], load_sem.at[0]),
        pltpu.make_async_copy(fine_hbm, fine_in, load_sem.at[1]),
        pltpu.make_async_copy(weight_hbm, weight_in, load_sem.at[2]),
        pltpu.make_async_copy(coarse_hbm.at[:, ROWS:BLOCK], pool_high.at[16:20], load_sem.at[3]),
    ]
    for copy in loads:
        copy.start()

    barrier = pltpu.get_barrier_semaphore()
    first_at = jnp.where(c == 0, z, y)
    third_at = jnp.where(c == 0, y, z)

    def first_peer(a):
        return at(gx, jnp.where(c == 0, a, z), jnp.where(c == 0, y, a), c)

    def third_peer(d):
        return at(gx, jnp.where(c == 0, z, d), jnp.where(c == 0, d, y), c)

    partners = [mate, away]
    for s in (1, 2, 3):
        partners += [first_peer((first_at + s) % 4), ((gx + s) % 4, gy), third_peer((third_at + s) % 4)]
    for who in partners:
        pl.semaphore_signal(barrier, inc=1, device_id=who, device_id_type=MESH)
    pl.semaphore_wait(barrier, len(partners))

    def remote(src, dst, send, recv, who):
        return pltpu.make_async_remote_copy(
            src_ref=src, dst_ref=dst, send_sem=send, recv_sem=recv, device_id=who, device_id_type=MESH
        )

    ORDER = [(h, j) for h in range(2) for j in range(2)]

    def own(h, j):
        return coarse_hbm.at[pl.ds(2 * j, 2), pl.ds(ROWS * h, ROWS)]

    def part(r, h, j):
        return pools[h].at[pl.ds(4 * r + 2 * j, 2)]

    def x_copy(i, h, j):
        who, r = (((gx + 1) % 4, gy), 1) if i == 0 else (((gx + 3) % 4, gy), 7)
        return remote(own(h, j), part(r, h, j), hx_send.at[i, h, j], hx_recv.at[i, h, j], who)

    def y_copy(i, p, h, j):
        who = (gx, (gy + jnp.where(i == 0, 1, 31)) % 32)
        src = own(h, j) if p == 1 else part(3 * p + 1, h, j)
        return remote(src, part(3 * p + 2 * i, h, j), hy_send.at[i, p, h, j], hy_recv.at[i, p, h, j], who)

    def corner_copy(p):
        who = ((gx + 1 + p) % 4, gy)
        src, dst = part(3 + 2 * c, 1, 1), part(3 * p + 2 * c, 1, 1)
        return remote(src, dst, hy_send.at[1 - c, p, 1, 1], hy_recv.at[c, p, 1, 1], who)

    def own_along_y(h, j):
        for i in range(2):
            y_copy(i, 1, h, j).start()

    for h, j in ORDER:
        for i in range(2):
            x_copy(i, h, j).start()
    own_along_y(0, 0)
    own_along_y(0, 1)
    own_along_y(1, 1)

    def forward(h, j):
        for p in (0, 2):
            x_copy(p // 2, h, j).wait_recv()
            if (h, j) == (1, 1):
                y_copy(c, p, h, j).start()
            else:
                for i in range(2):
                    y_copy(i, p, h, j).start()

    def halo_done(h):
        for j in range(2):
            for i in range(2):
                for p in range(3):
                    if (p, h, j) != (1, 1, 1):
                        y_copy(i, p, h, j).wait_recv()
                for p in (0, 2):
                    y_copy(i, p, h, j).wait_send()

        @pl.when(gx == 0)
        def _():
            pools[h][0:12] = jnp.zeros((12, ROWS, C), BF16)

        @pl.when(gx == 3)
        def _():
            pools[h][24:36] = jnp.zeros((12, ROWS, C), BF16)

        for edge, q in ((0, 0), (31, 2)):

            @pl.when(gy == edge)
            def _():
                for p in range(3):
                    r = 3 * p + q
                    pools[h][4 * r : 4 * r + 4] = jnp.zeros((4, ROWS, C), BF16)

    for pool in pools:
        pool[36] = jnp.zeros((ROWS, C), BF16)
    count = counts_ref[0, 0]
    loads[1].wait()
    for f in range(SLOTS // 4):
        blocks = [jnp.where(4 * f + i < count, fine_in[4 * f + i], jnp.zeros((), BF16)) for i in range(4)]
        for h in range(2):
            quad = jnp.concatenate([block[ROWS * h : ROWS * (h + 1)] for block in blocks], axis=0)
            fine_t[h, :, f * C : (f + 1) * C] = quad.T
    acc[:, K * C : K * C + 8, :] = jnp.zeros((2, 8, HALF), F32)
    from_mate[K * C : K * C + 8, :] = jnp.zeros((8, HALF), F32)
    loads[0].wait()
    loads[3].wait()
    loads[2].wait()

    def turn(k, carry):
        weight_t[pl.ds(pl.multiple_of(k * C, C), C), :] = weight_in[k].T
        return carry

    forward(0, 0)
    lax.fori_loop(0, 9, turn, 0)
    forward(0, 1)
    own_along_y(1, 0)
    for i in range(2):
        y_copy(i, 1, 1, 1).wait_recv()
    for p in (0, 2):
        corner_copy(p).start()
    lax.fori_loop(9, 18, turn, 0)
    forward(1, 0)
    lax.fori_loop(18, K, turn, 0)
    forward(1, 1)
    halo_done(0)

    def chosen(k, f):
        return jnp.clip(map_ref[f, k], 0, 36)

    def weight_offset(k, h):
        total = None
        for s in range(SLOTS // 4):
            quad = [pools[h][chosen(k, 4 * s + i)] for i in range(4)]
            piece = dot(fine_t[h, :, s * C : (s + 1) * C], jnp.concatenate(quad, axis=0))
            total = piece if total is None else total + piece
        return total * (1.0 / math.sqrt(262144))

    begin = (gx + 1) % 4
    begin = jnp.where(begin == 0, 0, jnp.where(begin == 1, 6, jnp.where(begin == 2, 13, 20)))

    def rows_of(n):
        return pl.ds(pl.multiple_of((begin + n) % K * C, C), C)

    def first_half(g, carry):
        for i in range(7):
            n = 7 * g + i
            total = weight_offset((begin + n) % K, 0)
            for side in range(2):
                acc[side, rows_of(n), :] = total[:, side * HALF : (side + 1) * HALF]
        return carry

    def mate_copy(n):
        rows = rows_of(n)
        return remote(acc.at[1 - c, rows], from_mate.at[rows], m_send.at[n], m_recv.at[n], mate)

    def members(g):
        return range(0 if g == 0 else ENDS[g - 1], ENDS[g])

    def weight_group(start, end):
        for n in range(start, end):
            total = weight_offset((begin + n) % K, 1)
            if n >= 21:
                total = total + weight_offset((begin + n) % K, 0)
            for side in range(2):
                piece = total[:, side * HALF : (side + 1) * HALF]
                acc[side, rows_of(n), :] = piece if n >= 21 else acc[side, rows_of(n), :] + piece
        for n in range(start, end):
            mate_copy(n).start()

    def summed_unit(g, a, d):
        start = UNIT * (16 * ((gx + 1 + g) % 4) + jnp.where(c == 0, 4 * a + d, 4 * d + a))
        return acc[c, pl.ds(start, LONG), :] + from_mate[pl.ds(start, LONG), :]

    def first_copy(g, s):
        who = first_peer((first_at + s) % 4)
        return remote(send1.at[s - 1, g], recv1.at[3 - s, g], s1_send.at[s - 1, g], s1_recv.at[3 - s, g], who)

    def first_stage(g):
        for n in members(g):
            mate_copy(n).wait_recv()
        for s in (2, 1, 3):
            for d in range(4):
                send1[s - 1, g, d] = encode(summed_unit(g, (first_at + s) % 4, d))
            first_copy(g, s).start()

    def second_copy(g):
        return remote(send2.at[g], recv2.at[g], s2_send.at[g], s2_recv.at[g], ((gx + 1 + g) % 4, gy))

    def third_copy(d):
        slot = (third_at - d + 4) % 4 - 1
        return remote(send3.at[d], recv3.at[slot], s3_send.at[d], s3_recv.at[slot], third_peer(d))

    def second_stage(g):
        for s in (1, 2, 3):
            first_copy(g, s).wait_recv()
        if g == 3:
            for slot in range(3):
                second_copy(slot).wait_recv()
        for d in range(4):
            summed = summed_unit(g, first_at, d)
            for slot in range(3):
                summed = summed + decode(recv1[slot, g, d])
            if g < 3:
                send2[g, d] = encode(summed)
                continue
            for slot in range(3):
                summed = summed + decode(recv2[slot, d])

            @pl.when(d == third_at)
            def _():
                total2[...] = summed

            @pl.when(d != third_at)
            def _():
                send3[d] = encode(summed)
                third_copy(d).start()

        if g < 3:
            second_copy(g).start()

    def fine_part(s, width):
        rows = []
        for f in range(width):
            for pool in pools:
                rows.append(jnp.concatenate([pool[chosen(k, s * width + f)] for k in range(K)], axis=1))
        got = dot(jnp.concatenate(rows, axis=0), weight_t[...]).astype(BF16)
        for f in range(width):
            slot = s * width + f
            fine_out[slot] = jnp.where(
                slot < count, got[f * BLOCK : (f + 1) * BLOCK], jnp.zeros((), BF16)
            )

    def fine_step(s):
        fine_part(s, 2)


    lax.fori_loop(0, 3, first_half, 0)
    halo_done(1)
    weight_group(0, 4)
    weight_group(4, 8)
    weight_group(8, 15)
    first_stage(0)
    weight_group(15, 21)
    first_stage(1)
    weight_group(21, 27)
    first_stage(2)
    fine_step(0)
    first_stage(3)
    second_stage(0)
    fine_step(1)
    fine_step(2)
    second_stage(1)
    fine_step(3)
    second_stage(2)
    fine_step(4)
    fine_step(5)
    second_stage(3)
    fine_step(6)
    fine_step(7)

    for h, j in ORDER:
        for i in range(2):
            x_copy(i, h, j).wait_send()
            y_copy(i, 1, h, j).wait_send()

    def drain_mate(n, carry):
        mate_copy(n).wait_send()
        return carry

    lax.fori_loop(0, K, drain_mate, 0)
    for g in range(4):
        for s in (1, 2, 3):
            first_copy(g, s).wait_send()

    summed = total2[...]
    for e in range(3):
        remote(recv3.at[e], recv3.at[e], s3_send.at[0], s3_recv.at[e], mate).wait_recv()
        summed = summed + decode(recv3[e])
    total3[...] = summed

    own_rows[0:MINE, :] = total3[pl.ds(MINE * (1 - c), MINE), :]
    last = remote(own_rows, mate_rows, f_sem.at[0], f_sem.at[1], mate)
    last.start()
    weight_out[:, pl.ds(pl.multiple_of(c * HALF, HALF), HALF)] = total3[pl.ds(MINE * c, MINE), :]
    last.wait_recv()
    weight_out[:, pl.ds(pl.multiple_of((1 - c) * HALF, HALF), HALF)] = mate_rows[0:MINE, :]

    for g in range(4):
        if g < 3:
            second_copy(g).wait_send()

        @pl.when(g != third_at)
        def _():
            third_copy(g).wait_send()

    last.wait_send()


def finish(fine_in, weight_in, fine_out, weight_out, sems):
    copies = [pltpu.make_async_copy(weight_in, weight_out, sems.at[4])]
    for s in range(4):
        rows = pl.ds(4 * s, 4)
        copies.append(pltpu.make_async_copy(fine_in.at[rows], fine_out.at[rows], sems.at[s]))
    for copy in copies:
        copy.start()
    for copy in copies:
        copy.wait()


def local(fine_feat, coarse_grad, kernel_map, counts, weight):
    anywhere = pl.BlockSpec(memory_space=pl.ANY)
    smem = pl.BlockSpec(memory_space=pltpu.SMEM)
    vmem = pl.BlockSpec(memory_space=pltpu.VMEM)
    dma = pltpu.SemaphoreType.DMA
    fine, weight_grad = pl.pallas_call(
        kernel,
        out_shape=(pltpu.VMEM((SLOTS, BLOCK, C), BF16), pltpu.VMEM((MINE, C), F32)),
        in_specs=[anywhere, anywhere, smem, smem, anywhere],
        out_specs=(vmem, vmem),
        scratch_shapes=[
            pltpu.VMEM((37, ROWS, C), BF16),
            pltpu.VMEM((37, ROWS, C), BF16),
            pltpu.VMEM((SLOTS, BLOCK, C), BF16),
            pltpu.VMEM((2, C, SLOTS * ROWS), BF16),
            pltpu.VMEM((K, C, C), BF16),
            pltpu.VMEM((K * C, C), BF16),
            pltpu.VMEM((2, K * C + 8, HALF), F32),
            pltpu.VMEM((K * C + 8, HALF), F32),
            pltpu.VMEM((3, 4, 4, LONG, HALF), I16),
            pltpu.VMEM((3, 4, 4, LONG, HALF), I16),
            pltpu.VMEM((3, 4, LONG, HALF), I16),
            pltpu.VMEM((3, 4, LONG, HALF), I16),
            pltpu.VMEM((4, LONG, HALF), I16),
            pltpu.VMEM((3, LONG, HALF), I16),
            pltpu.VMEM((LONG, HALF), F32),
            pltpu.VMEM((LONG, HALF), F32),
            pltpu.VMEM((56, HALF), F32),
            pltpu.VMEM((56, HALF), F32),
            dma((4,)), dma((2, 2, 2)), dma((2, 2, 2)), dma((2, 3, 2, 2)), dma((2, 3, 2, 2)), dma((K,)), dma((K,)),
            dma((3, 4)), dma((3, 4)), dma((3,)), dma((3,)), dma((4,)), dma((3,)), dma((2,)),
        ],
        compiler_params=pltpu.CompilerParams(
            collective_id=0, has_side_effects=True, vmem_limit_bytes=56 << 20
        ),
        cost_estimate=pl.CostEstimate(flops=14_500_000_000, bytes_accessed=8_000_000, transcendentals=0),
    )(fine_feat[0, 0], coarse_grad[0, 0], kernel_map[0, 0].T, counts, weight)
    fine, weight_grad = pl.pallas_call(
        finish,
        out_shape=(
            jax.ShapeDtypeStruct((SLOTS, BLOCK, C), BF16),
            jax.ShapeDtypeStruct((MINE, C), F32),
        ),
        in_specs=[vmem, vmem],
        out_specs=(anywhere, anywhere),
        scratch_shapes=[dma((5,))],
        compiler_params=pltpu.CompilerParams(vmem_limit_bytes=8 << 20),
    )(fine, weight_grad)
    return fine[None, None], weight_grad


def solution(mesh):
    return jax.shard_map(
        local,
        mesh=mesh,
        in_specs=(
            P("gx", "gy", None, None, None),
            P("gx", "gy", None, None, None),
            P("gx", "gy", None, None),
            P("gx", "gy"),
            P(),
        ),
        out_specs=(P("gx", "gy", None, None, None), P(("gx", "gy"), None)),
        check_vma=False,
    )
```

```python
import functools
import math

import jax
import jax.numpy as jnp
from jax import lax
from jax.experimental import pallas as pl
from jax.experimental.pallas import tpu as pltpu
from jax.sharding import PartitionSpec as P

MESH = pl.DeviceIdType.MESH
F32, BF16, I16 = jnp.float32, jnp.bfloat16, jnp.int16
K, C, BLOCK, SLOTS, COARSE = 27, 256, 128, 16, 4
HALF = C // 2
ENDS = (8, 15, 21, 27)
UNIT = 108
LONG = 112
MINE = 54
ROWS = 64
LEVELS = 32767.0

dot = functools.partial(jnp.dot, preferred_element_type=F32)


def encode(values):
    held = lax.broadcasted_iota(jnp.int32, (LONG, HALF), 0) < UNIT
    top = jnp.max(jnp.where(held, jnp.abs(values), 0.0), axis=0, keepdims=True)
    power = jnp.ceil(jnp.log2(jnp.maximum(top, 1e-35)) + 1e-3)
    codes = jnp.floor(values * (jnp.exp2(-power) * LEVELS) + 0.5)
    return jnp.where(held, codes, power).astype(jnp.int32).astype(I16)


def decode(unit):
    codes = unit.astype(jnp.int32).astype(F32)
    return codes * (jnp.exp2(codes[UNIT : UNIT + 1, :]) * (1.0 / LEVELS))


def kernel(
    fine_hbm, coarse_hbm, map_ref, counts_ref, weight_hbm,
    fine_out, weight_out,
    pool_low, pool_high, fine_in, fine_t, weight_in, weight_t, acc, from_mate,
    send1, recv1, send2, recv2, send3, recv3, total2, total3,
    own_rows, mate_rows,
    load_sem, hx_send, hx_recv, hy_send, hy_recv, m_send, m_recv,
    s1_send, s1_recv, s2_send, s2_recv, s3_send, s3_recv, f_sem,
):
    pools = (pool_low, pool_high)
    gx, gy = lax.axis_index("gx"), lax.axis_index("gy")
    z, y, c = gy // 8, (gy // 2) % 4, gy % 2

    def at(x_, z_, y_, c_):
        return (x_, z_ * 8 + y_ * 2 + c_)

    mate = at(gx, z, y, 1 - c)
    up, down = (gx, (gy + 1) % 32), (gx, (gy + 31) % 32)
    away = (gx, (gy + jnp.where(c == 0, 31, 1)) % 32)

    loads = [
        pltpu.make_async_copy(coarse_hbm.at[:, 0:ROWS], pool_low.at[16:20], load_sem.at[0]),
        pltpu.make_async_copy(fine_hbm, fine_in, load_sem.at[1]),
        pltpu.make_async_copy(weight_hbm, weight_in, load_sem.at[2]),
        pltpu.make_async_copy(coarse_hbm.at[:, ROWS:BLOCK], pool_high.at[16:20], load_sem.at[3]),
    ]
    for copy in loads:
        copy.start()

    barrier = pltpu.get_barrier_semaphore()
    first_at = jnp.where(c == 0, z, y)
    third_at = jnp.where(c == 0, y, z)

    def first_peer(a):
        return at(gx, jnp.where(c == 0, a, z), jnp.where(c == 0, y, a), c)

    def third_peer(d):
        return at(gx, jnp.where(c == 0, z, d), jnp.where(c == 0, d, y), c)

    partners = [mate, away]
    for s in (1, 2, 3):
        partners += [first_peer((first_at + s) % 4), ((gx + s) % 4, gy), third_peer((third_at + s) % 4)]
    for who in partners:
        pl.semaphore_signal(barrier, inc=1, device_id=who, device_id_type=MESH)
    pl.semaphore_wait(barrier, len(partners))

    def remote(src, dst, send, recv, who):
        return pltpu.make_async_remote_copy(
            src_ref=src, dst_ref=dst, send_sem=send, recv_sem=recv, device_id=who, device_id_type=MESH
        )

    ORDER = [(h, j) for h in range(2) for j in range(2)]

    def own(h, j):
        return coarse_hbm.at[pl.ds(2 * j, 2), pl.ds(ROWS * h, ROWS)]

    def part(r, h, j):
        return pools[h].at[pl.ds(4 * r + 2 * j, 2)]

    def x_copy(i, h, j):
        who, r = (((gx + 1) % 4, gy), 1) if i == 0 else (((gx + 3) % 4, gy), 7)
        return remote(own(h, j), part(r, h, j), hx_send.at[i, h, j], hx_recv.at[i, h, j], who)

    def y_copy(i, p, h, j):
        who = (gx, (gy + jnp.where(i == 0, 1, 31)) % 32)
        src = own(h, j) if p == 1 else part(3 * p + 1, h, j)
        return remote(src, part(3 * p + 2 * i, h, j), hy_send.at[i, p, h, j], hy_recv.at[i, p, h, j], who)

    def corner_copy(p):
        who = ((gx + 1 + p) % 4, gy)
        src, dst = part(3 + 2 * c, 1, 1), part(3 * p + 2 * c, 1, 1)
        return remote(src, dst, hy_send.at[1 - c, p, 1, 1], hy_recv.at[c, p, 1, 1], who)

    def own_along_y(h, j):
        for i in range(2):
            y_copy(i, 1, h, j).start()

    for h, j in ORDER:
        for i in range(2):
            x_copy(i, h, j).start()
    own_along_y(0, 0)
    own_along_y(0, 1)
    own_along_y(1, 1)

    def forward(h, j):
        for p in (0, 2):
            x_copy(p // 2, h, j).wait_recv()
            if (h, j) == (1, 1):
                y_copy(c, p, h, j).start()
            else:
                for i in range(2):
                    y_copy(i, p, h, j).start()

    def halo_done(h):
        for j in range(2):
            for i in range(2):
                for p in range(3):
                    if (p, h, j) != (1, 1, 1):
                        y_copy(i, p, h, j).wait_recv()
                for p in (0, 2):
                    y_copy(i, p, h, j).wait_send()

        @pl.when(gx == 0)
        def _():
            pools[h][0:12] = jnp.zeros((12, ROWS, C), BF16)

        @pl.when(gx == 3)
        def _():
            pools[h][24:36] = jnp.zeros((12, ROWS, C), BF16)

        for edge, q in ((0, 0), (31, 2)):

            @pl.when(gy == edge)
            def _():
                for p in range(3):
                    r = 3 * p + q
                    pools[h][4 * r : 4 * r + 4] = jnp.zeros((4, ROWS, C), BF16)

    for pool in pools:
        pool[36] = jnp.zeros((ROWS, C), BF16)
    count = counts_ref[0, 0]
    loads[1].wait()
    for f in range(SLOTS // 4):
        blocks = [jnp.where(4 * f + i < count, fine_in[4 * f + i], jnp.zeros((), BF16)) for i in range(4)]
        for h in range(2):
            quad = jnp.concatenate([block[ROWS * h : ROWS * (h + 1)] for block in blocks], axis=0)
            fine_t[h, :, f * C : (f + 1) * C] = quad.T
    acc[:, K * C : K * C + 8, :] = jnp.zeros((2, 8, HALF), F32)
    from_mate[K * C : K * C + 8, :] = jnp.zeros((8, HALF), F32)
    loads[0].wait()
    loads[3].wait()
    loads[2].wait()

    def turn(k, carry):
        weight_t[pl.ds(pl.multiple_of(k * C, C), C), :] = weight_in[k].T
        return carry

    forward(0, 0)
    forward(0, 1)
    own_along_y(1, 0)
    for i in range(2):
        y_copy(i, 1, 1, 1).wait_recv()
    for p in (0, 2):
        corner_copy(p).start()
    lax.fori_loop(0, 14, turn, 0)
    forward(1, 0)
    lax.fori_loop(14, K, turn, 0)
    forward(1, 1)
    halo_done(0)

    def chosen(k, f):
        return jnp.clip(map_ref[f, k], 0, 36)

    def weight_offset(k, h):
        total = None
        for s in range(SLOTS // 4):
            quad = [pools[h][chosen(k, 4 * s + i)] for i in range(4)]
            piece = dot(fine_t[h, :, s * C : (s + 1) * C], jnp.concatenate(quad, axis=0))
            total = piece if total is None else total + piece
        return total * (1.0 / math.sqrt(262144))

    begin = (gx + 1) % 4
    begin = jnp.where(begin == 0, 0, jnp.where(begin == 1, 6, jnp.where(begin == 2, 13, 20)))

    def rows_of(n):
        return pl.ds(pl.multiple_of((begin + n) % K * C, C), C)

    def first_half(g, carry):
        for i in range(7):
            n = 7 * g + i
            total = weight_offset((begin + n) % K, 0)
            for side in range(2):
                acc[side, rows_of(n), :] = total[:, side * HALF : (side + 1) * HALF]
        return carry

    def mate_copy(n):
        rows = rows_of(n)
        return remote(acc.at[1 - c, rows], from_mate.at[rows], m_send.at[n], m_recv.at[n], mate)

    def members(g):
        return range(0 if g == 0 else ENDS[g - 1], ENDS[g])

    def weight_group(start, end):
        for n in range(start, end):
            total = weight_offset((begin + n) % K, 1)
            if n >= 21:
                total = total + weight_offset((begin + n) % K, 0)
            for side in range(2):
                piece = total[:, side * HALF : (side + 1) * HALF]
                acc[side, rows_of(n), :] = piece if n >= 21 else acc[side, rows_of(n), :] + piece
        for n in range(start, end):
            mate_copy(n).start()

    def summed_unit(g, a, d):
        start = UNIT * (16 * ((gx + 1 + g) % 4) + jnp.where(c == 0, 4 * a + d, 4 * d + a))
        return acc[c, pl.ds(start, LONG), :] + from_mate[pl.ds(start, LONG), :]

    def first_copy(g, s):
        who = first_peer((first_at + s) % 4)
        return remote(send1.at[s - 1, g], recv1.at[3 - s, g], s1_send.at[s - 1, g], s1_recv.at[3 - s, g], who)

    def first_stage(g):
        for n in members(g):
            mate_copy(n).wait_recv()
        for s in (2, 1, 3):
            for d in range(4):
                send1[s - 1, g, d] = encode(summed_unit(g, (first_at + s) % 4, d))
            first_copy(g, s).start()

    def second_copy(g):
        return remote(send2.at[g], recv2.at[g], s2_send.at[g], s2_recv.at[g], ((gx + 1 + g) % 4, gy))

    def third_copy(d):
        slot = (third_at - d + 4) % 4 - 1
        return remote(send3.at[d], recv3.at[slot], s3_send.at[d], s3_recv.at[slot], third_peer(d))

    def second_stage(g):
        for s in (1, 2, 3):
            first_copy(g, s).wait_recv()
        if g == 3:
            for slot in range(3):
                second_copy(slot).wait_recv()
        for d in range(4):
            summed = summed_unit(g, first_at, d)
            for slot in range(3):
                summed = summed + decode(recv1[slot, g, d])
            if g < 3:
                send2[g, d] = encode(summed)
                continue
            for slot in range(3):
                summed = summed + decode(recv2[slot, d])

            @pl.when(d == third_at)
            def _():
                total2[...] = summed

            @pl.when(d != third_at)
            def _():
                send3[d] = encode(summed)
                third_copy(d).start()

        if g < 3:
            second_copy(g).start()

    def fine_part(s, width):
        rows = []
        for f in range(width):
            for pool in pools:
                rows.append(jnp.concatenate([pool[chosen(k, s * width + f)] for k in range(K)], axis=1))
        got = dot(jnp.concatenate(rows, axis=0), weight_t[...]).astype(BF16)
        for f in range(width):
            slot = s * width + f
            fine_out[slot] = jnp.where(
                slot < count, got[f * BLOCK : (f + 1) * BLOCK], jnp.zeros((), BF16)
            )

    def fine_step(s):
        fine_part(s, 2)


    lax.fori_loop(0, 3, first_half, 0)
    halo_done(1)
    weight_group(0, 4)
    weight_group(4, 8)
    weight_group(8, 15)
    first_stage(0)
    weight_group(15, 21)
    first_stage(1)
    weight_group(21, 27)
    first_stage(2)
    fine_step(0)
    first_stage(3)
    second_stage(0)
    fine_step(1)
    fine_step(2)
    second_stage(1)
    fine_step(3)
    second_stage(2)
    fine_step(4)
    fine_step(5)
    second_stage(3)
    fine_step(6)
    fine_step(7)

    for h, j in ORDER:
        for i in range(2):
            x_copy(i, h, j).wait_send()
            y_copy(i, 1, h, j).wait_send()

    def drain_mate(n, carry):
        mate_copy(n).wait_send()
        return carry

    lax.fori_loop(0, K, drain_mate, 0)
    for g in range(4):
        for s in (1, 2, 3):
            first_copy(g, s).wait_send()

    summed = total2[...]
    for e in range(3):
        remote(recv3.at[e], recv3.at[e], s3_send.at[0], s3_recv.at[e], mate).wait_recv()
        summed = summed + decode(recv3[e])
    total3[...] = summed

    own_rows[0:MINE, :] = total3[pl.ds(MINE * (1 - c), MINE), :]
    last = remote(own_rows, mate_rows, f_sem.at[0], f_sem.at[1], mate)
    last.start()
    weight_out[:, pl.ds(pl.multiple_of(c * HALF, HALF), HALF)] = total3[pl.ds(MINE * c, MINE), :]
    last.wait_recv()
    weight_out[:, pl.ds(pl.multiple_of((1 - c) * HALF, HALF), HALF)] = mate_rows[0:MINE, :]

    for g in range(4):
        if g < 3:
            second_copy(g).wait_send()

        @pl.when(g != third_at)
        def _():
            third_copy(g).wait_send()

    last.wait_send()


def finish(fine_in, weight_in, fine_out, weight_out, sems):
    copies = [pltpu.make_async_copy(weight_in, weight_out, sems.at[4])]
    for s in range(4):
        rows = pl.ds(4 * s, 4)
        copies.append(pltpu.make_async_copy(fine_in.at[rows], fine_out.at[rows], sems.at[s]))
    for copy in copies:
        copy.start()
    for copy in copies:
        copy.wait()


def local(fine_feat, coarse_grad, kernel_map, counts, weight):
    anywhere = pl.BlockSpec(memory_space=pl.ANY)
    smem = pl.BlockSpec(memory_space=pltpu.SMEM)
    vmem = pl.BlockSpec(memory_space=pltpu.VMEM)
    dma = pltpu.SemaphoreType.DMA
    fine, weight_grad = pl.pallas_call(
        kernel,
        out_shape=(pltpu.VMEM((SLOTS, BLOCK, C), BF16), pltpu.VMEM((MINE, C), F32)),
        in_specs=[anywhere, anywhere, smem, smem, anywhere],
        out_specs=(vmem, vmem),
        scratch_shapes=[
            pltpu.VMEM((37, ROWS, C), BF16),
            pltpu.VMEM((37, ROWS, C), BF16),
            pltpu.VMEM((SLOTS, BLOCK, C), BF16),
            pltpu.VMEM((2, C, SLOTS * ROWS), BF16),
            pltpu.VMEM((K, C, C), BF16),
            pltpu.VMEM((K * C, C), BF16),
            pltpu.VMEM((2, K * C + 8, HALF), F32),
            pltpu.VMEM((K * C + 8, HALF), F32),
            pltpu.VMEM((3, 4, 4, LONG, HALF), I16),
            pltpu.VMEM((3, 4, 4, LONG, HALF), I16),
            pltpu.VMEM((3, 4, LONG, HALF), I16),
            pltpu.VMEM((3, 4, LONG, HALF), I16),
            pltpu.VMEM((4, LONG, HALF), I16),
            pltpu.VMEM((3, LONG, HALF), I16),
            pltpu.VMEM((LONG, HALF), F32),
            pltpu.VMEM((LONG, HALF), F32),
            pltpu.VMEM((56, HALF), F32),
            pltpu.VMEM((56, HALF), F32),
            dma((4,)), dma((2, 2, 2)), dma((2, 2, 2)), dma((2, 3, 2, 2)), dma((2, 3, 2, 2)), dma((K,)), dma((K,)),
            dma((3, 4)), dma((3, 4)), dma((3,)), dma((3,)), dma((4,)), dma((3,)), dma((2,)),
        ],
        compiler_params=pltpu.CompilerParams(
            collective_id=0, has_side_effects=True, vmem_limit_bytes=56 << 20
        ),
        cost_estimate=pl.CostEstimate(flops=14_500_000_000, bytes_accessed=8_000_000, transcendentals=0),
    )(fine_feat[0, 0], coarse_grad[0, 0], kernel_map[0, 0].T, counts, weight)
    fine, weight_grad = pl.pallas_call(
        finish,
        out_shape=(
            jax.ShapeDtypeStruct((SLOTS, BLOCK, C), BF16),
            jax.ShapeDtypeStruct((MINE, C), F32),
        ),
        in_specs=[vmem, vmem],
        out_specs=(anywhere, anywhere),
        scratch_shapes=[dma((5,))],
        compiler_params=pltpu.CompilerParams(vmem_limit_bytes=8 << 20),
    )(fine, weight_grad)
    return fine[None, None], weight_grad


def solution(mesh):
    return jax.shard_map(
        local,
        mesh=mesh,
        in_specs=(
            P("gx", "gy", None, None, None),
            P("gx", "gy", None, None, None),
            P("gx", "gy", None, None),
            P("gx", "gy"),
            P(),
        ),
        out_specs=(P("gx", "gy", None, None, None), P(("gx", "gy"), None)),
        check_vma=False,
    )
```

```python
import functools
import math

import jax
import jax.numpy as jnp
from jax import lax
from jax.experimental import pallas as pl
from jax.experimental.pallas import tpu as pltpu
from jax.sharding import PartitionSpec as P

MESH = pl.DeviceIdType.MESH
F32, BF16, I16 = jnp.float32, jnp.bfloat16, jnp.int16
K, C, BLOCK, SLOTS, COARSE = 27, 256, 128, 16, 4
HALF = C // 2
ENDS = (8, 15, 21, 27)
UNIT = 108
LONG = 112
MINE = 54
ROWS = 64
LEVELS = 32767.0

dot = functools.partial(jnp.dot, preferred_element_type=F32)


def encode(values):
    held = lax.broadcasted_iota(jnp.int32, (LONG, HALF), 0) < UNIT
    top = jnp.max(jnp.where(held, jnp.abs(values), 0.0), axis=0, keepdims=True)
    power = jnp.ceil(jnp.log2(jnp.maximum(top, 1e-35)) + 1e-3)
    codes = jnp.floor(values * (jnp.exp2(-power) * LEVELS) + 0.5)
    return jnp.where(held, codes, power).astype(jnp.int32).astype(I16)


def decode(unit):
    codes = unit.astype(jnp.int32).astype(F32)
    return codes * (jnp.exp2(codes[UNIT : UNIT + 1, :]) * (1.0 / LEVELS))


def kernel(
    fine_hbm, coarse_hbm, map_ref, counts_ref, weight_hbm,
    fine_out, weight_out,
    pool_low, pool_high, fine_in, fine_t, weight_in, weight_t, acc, from_mate,
    send1, recv1, send2, recv2, send3, recv3, total2, total3,
    own_rows, mate_rows,
    load_sem, hx_send, hx_recv, hy_send, hy_recv, m_send, m_recv,
    s1_send, s1_recv, s2_send, s2_recv, s3_send, s3_recv, f_sem,
):
    pools = (pool_low, pool_high)
    gx, gy = lax.axis_index("gx"), lax.axis_index("gy")
    z, y, c = gy // 8, (gy // 2) % 4, gy % 2

    def at(x_, z_, y_, c_):
        return (x_, z_ * 8 + y_ * 2 + c_)

    mate = at(gx, z, y, 1 - c)
    up, down = (gx, (gy + 1) % 32), (gx, (gy + 31) % 32)
    away = (gx, (gy + jnp.where(c == 0, 31, 1)) % 32)

    loads = [
        pltpu.make_async_copy(coarse_hbm.at[:, 0:ROWS], pool_low.at[16:20], load_sem.at[0]),
        pltpu.make_async_copy(fine_hbm, fine_in, load_sem.at[1]),
        pltpu.make_async_copy(weight_hbm, weight_in, load_sem.at[2]),
        pltpu.make_async_copy(coarse_hbm.at[:, ROWS:BLOCK], pool_high.at[16:20], load_sem.at[3]),
    ]
    for copy in loads:
        copy.start()

    barrier = pltpu.get_barrier_semaphore()
    first_at = jnp.where(c == 0, z, y)
    third_at = jnp.where(c == 0, y, z)

    def first_peer(a):
        return at(gx, jnp.where(c == 0, a, z), jnp.where(c == 0, y, a), c)

    def third_peer(d):
        return at(gx, jnp.where(c == 0, z, d), jnp.where(c == 0, d, y), c)

    partners = [mate, away]
    for s in (1, 2, 3):
        partners += [first_peer((first_at + s) % 4), ((gx + s) % 4, gy), third_peer((third_at + s) % 4)]
    for who in partners:
        pl.semaphore_signal(barrier, inc=1, device_id=who, device_id_type=MESH)
    pl.semaphore_wait(barrier, len(partners))

    def remote(src, dst, send, recv, who):
        return pltpu.make_async_remote_copy(
            src_ref=src, dst_ref=dst, send_sem=send, recv_sem=recv, device_id=who, device_id_type=MESH
        )

    ORDER = [(h, j) for h in range(2) for j in range(2)]

    def own(h, j):
        return coarse_hbm.at[pl.ds(2 * j, 2), pl.ds(ROWS * h, ROWS)]

    def part(r, h, j):
        return pools[h].at[pl.ds(4 * r + 2 * j, 2)]

    def x_copy(i, h, j):
        who, r = (((gx + 1) % 4, gy), 1) if i == 0 else (((gx + 3) % 4, gy), 7)
        return remote(own(h, j), part(r, h, j), hx_send.at[i, h, j], hx_recv.at[i, h, j], who)

    def y_copy(i, p, h, j):
        who = (gx, (gy + jnp.where(i == 0, 1, 31)) % 32)
        src = own(h, j) if p == 1 else part(3 * p + 1, h, j)
        return remote(src, part(3 * p + 2 * i, h, j), hy_send.at[i, p, h, j], hy_recv.at[i, p, h, j], who)

    def corner_copy(p):
        who = ((gx + 1 + p) % 4, gy)
        src, dst = part(3 + 2 * c, 1, 1), part(3 * p + 2 * c, 1, 1)
        return remote(src, dst, hy_send.at[1 - c, p, 1, 1], hy_recv.at[c, p, 1, 1], who)

    def own_along_y(h, j):
        for i in range(2):
            y_copy(i, 1, h, j).start()

    for h, j in ORDER:
        for i in range(2):
            x_copy(i, h, j).start()
    own_along_y(0, 0)
    own_along_y(0, 1)
    own_along_y(1, 1)

    def forward(h, j):
        for p in (0, 2):
            x_copy(p // 2, h, j).wait_recv()
            if (h, j) == (1, 1):
                y_copy(c, p, h, j).start()
            else:
                for i in range(2):
                    y_copy(i, p, h, j).start()

    def halo_done(h):
        for j in range(2):
            for i in range(2):
                for p in range(3):
                    if (p, h, j) != (1, 1, 1):
                        y_copy(i, p, h, j).wait_recv()
                for p in (0, 2):
                    y_copy(i, p, h, j).wait_send()

        @pl.when(gx == 0)
        def _():
            pools[h][0:12] = jnp.zeros((12, ROWS, C), BF16)

        @pl.when(gx == 3)
        def _():
            pools[h][24:36] = jnp.zeros((12, ROWS, C), BF16)

        for edge, q in ((0, 0), (31, 2)):

            @pl.when(gy == edge)
            def _():
                for p in range(3):
                    r = 3 * p + q
                    pools[h][4 * r : 4 * r + 4] = jnp.zeros((4, ROWS, C), BF16)

    for pool in pools:
        pool[36] = jnp.zeros((ROWS, C), BF16)
    count = counts_ref[0, 0]
    loads[1].wait()
    for f in range(SLOTS // 4):
        blocks = [jnp.where(4 * f + i < count, fine_in[4 * f + i], jnp.zeros((), BF16)) for i in range(4)]
        for h in range(2):
            quad = jnp.concatenate([block[ROWS * h : ROWS * (h + 1)] for block in blocks], axis=0)
            fine_t[h, :, f * C : (f + 1) * C] = quad.T
    acc[:, K * C : K * C + 8, :] = jnp.zeros((2, 8, HALF), F32)
    from_mate[K * C : K * C + 8, :] = jnp.zeros((8, HALF), F32)
    loads[0].wait()
    loads[3].wait()
    loads[2].wait()

    def turn(k, carry):
        weight_t[pl.ds(pl.multiple_of(k * C, C), C), :] = weight_in[k].T
        return carry

    forward(0, 0)
    forward(0, 1)
    own_along_y(1, 0)
    for i in range(2):
        y_copy(i, 1, 1, 1).wait_recv()
    for p in (0, 2):
        corner_copy(p).start()
    lax.fori_loop(0, 14, turn, 0)
    forward(1, 0)
    lax.fori_loop(14, K, turn, 0)
    forward(1, 1)
    halo_done(0)

    def chosen(k, f):
        return jnp.clip(map_ref[f, k], 0, 36)

    def weight_offset(k, h):
        total = None
        for s in range(SLOTS // 4):
            quad = [pools[h][chosen(k, 4 * s + i)] for i in range(4)]
            piece = dot(fine_t[h, :, s * C : (s + 1) * C], jnp.concatenate(quad, axis=0))
            total = piece if total is None else total + piece
        return total * (1.0 / math.sqrt(262144))

    begin = (gx + 1) % 4
    begin = jnp.where(begin == 0, 0, jnp.where(begin == 1, 6, jnp.where(begin == 2, 13, 20)))

    def rows_of(n):
        return pl.ds(pl.multiple_of((begin + n) % K * C, C), C)

    def first_half(g, carry):
        for i in range(7):
            n = 7 * g + i
            total = weight_offset((begin + n) % K, 0)
            for side in range(2):
                acc[side, rows_of(n), :] = total[:, side * HALF : (side + 1) * HALF]
        return carry

    def mate_copy(n):
        rows = rows_of(n)
        return remote(acc.at[1 - c, rows], from_mate.at[rows], m_send.at[n], m_recv.at[n], mate)

    def members(g):
        return range(0 if g == 0 else ENDS[g - 1], ENDS[g])

    def weight_group(start, end):
        for n in range(start, end):
            total = weight_offset((begin + n) % K, 1)
            if n >= 21:
                total = total + weight_offset((begin + n) % K, 0)
            for side in range(2):
                piece = total[:, side * HALF : (side + 1) * HALF]
                acc[side, rows_of(n), :] = piece if n >= 21 else acc[side, rows_of(n), :] + piece
        for n in range(start, end):
            mate_copy(n).start()

    def summed_unit(g, a, d):
        start = UNIT * (16 * ((gx + 1 + g) % 4) + jnp.where(c == 0, 4 * a + d, 4 * d + a))
        return acc[c, pl.ds(start, LONG), :] + from_mate[pl.ds(start, LONG), :]

    def first_copy(g, s):
        who = first_peer((first_at + s) % 4)
        return remote(send1.at[s - 1, g], recv1.at[3 - s, g], s1_send.at[s - 1, g], s1_recv.at[3 - s, g], who)

    def first_stage(g):
        for n in members(g):
            mate_copy(n).wait_recv()
        for s in (2, 1, 3):
            for d in range(4):
                send1[s - 1, g, d] = encode(summed_unit(g, (first_at + s) % 4, d))
            first_copy(g, s).start()

    def second_copy(g):
        return remote(send2.at[g], recv2.at[g], s2_send.at[g], s2_recv.at[g], ((gx + 1 + g) % 4, gy))

    def third_copy(d):
        slot = (third_at - d + 4) % 4 - 1
        return remote(send3.at[d], recv3.at[slot], s3_send.at[d], s3_recv.at[slot], third_peer(d))

    def second_stage(g):
        for s in (1, 2, 3):
            first_copy(g, s).wait_recv()
        if g == 3:
            for slot in range(3):
                second_copy(slot).wait_recv()
        for d in range(4):
            summed = summed_unit(g, first_at, d)
            for slot in range(3):
                summed = summed + decode(recv1[slot, g, d])
            if g < 3:
                send2[g, d] = encode(summed)
                continue
            for slot in range(3):
                summed = summed + decode(recv2[slot, d])

            @pl.when(d == third_at)
            def _():
                total2[...] = summed

            @pl.when(d != third_at)
            def _():
                send3[d] = encode(summed)
                third_copy(d).start()

        if g < 3:
            second_copy(g).start()

    def fine_part(s, width):
        rows = []
        for f in range(width):
            for pool in pools:
                rows.append(jnp.concatenate([pool[chosen(k, s * width + f)] for k in range(K)], axis=1))
        got = dot(jnp.concatenate(rows, axis=0), weight_t[...]).astype(BF16)
        for f in range(width):
            slot = s * width + f
            fine_out[slot] = jnp.where(
                slot < count, got[f * BLOCK : (f + 1) * BLOCK], jnp.zeros((), BF16)
            )

    def fine_step(s):
        fine_part(s, 4)


    lax.fori_loop(0, 3, first_half, 0)
    halo_done(1)
    weight_group(0, 4)
    weight_group(4, 8)
    weight_group(8, 15)
    first_stage(0)
    weight_group(15, 21)
    first_stage(1)
    weight_group(21, 27)
    first_stage(2)
    fine_step(0)
    first_stage(3)
    second_stage(0)
    fine_step(1)
    second_stage(1)
    second_stage(2)
    fine_step(2)
    second_stage(3)
    fine_step(3)

    for h, j in ORDER:
        for i in range(2):
            x_copy(i, h, j).wait_send()
            y_copy(i, 1, h, j).wait_send()

    def drain_mate(n, carry):
        mate_copy(n).wait_send()
        return carry

    lax.fori_loop(0, K, drain_mate, 0)
    for g in range(4):
        for s in (1, 2, 3):
            first_copy(g, s).wait_send()

    summed = total2[...]
    for e in range(3):
        remote(recv3.at[e], recv3.at[e], s3_send.at[0], s3_recv.at[e], mate).wait_recv()
        summed = summed + decode(recv3[e])
    total3[...] = summed

    own_rows[0:MINE, :] = total3[pl.ds(MINE * (1 - c), MINE), :]
    last = remote(own_rows, mate_rows, f_sem.at[0], f_sem.at[1], mate)
    last.start()
    weight_out[:, pl.ds(pl.multiple_of(c * HALF, HALF), HALF)] = total3[pl.ds(MINE * c, MINE), :]
    last.wait_recv()
    weight_out[:, pl.ds(pl.multiple_of((1 - c) * HALF, HALF), HALF)] = mate_rows[0:MINE, :]

    for g in range(4):
        if g < 3:
            second_copy(g).wait_send()

        @pl.when(g != third_at)
        def _():
            third_copy(g).wait_send()

    last.wait_send()


def finish(fine_in, weight_in, fine_out, weight_out, sems):
    copies = [pltpu.make_async_copy(weight_in, weight_out, sems.at[4])]
    for s in range(4):
        rows = pl.ds(4 * s, 4)
        copies.append(pltpu.make_async_copy(fine_in.at[rows], fine_out.at[rows], sems.at[s]))
    for copy in copies:
        copy.start()
    for copy in copies:
        copy.wait()


def local(fine_feat, coarse_grad, kernel_map, counts, weight):
    anywhere = pl.BlockSpec(memory_space=pl.ANY)
    smem = pl.BlockSpec(memory_space=pltpu.SMEM)
    vmem = pl.BlockSpec(memory_space=pltpu.VMEM)
    dma = pltpu.SemaphoreType.DMA
    fine, weight_grad = pl.pallas_call(
        kernel,
        out_shape=(pltpu.VMEM((SLOTS, BLOCK, C), BF16), pltpu.VMEM((MINE, C), F32)),
        in_specs=[anywhere, anywhere, smem, smem, anywhere],
        out_specs=(vmem, vmem),
        scratch_shapes=[
            pltpu.VMEM((37, ROWS, C), BF16),
            pltpu.VMEM((37, ROWS, C), BF16),
            pltpu.VMEM((SLOTS, BLOCK, C), BF16),
            pltpu.VMEM((2, C, SLOTS * ROWS), BF16),
            pltpu.VMEM((K, C, C), BF16),
            pltpu.VMEM((K * C, C), BF16),
            pltpu.VMEM((2, K * C + 8, HALF), F32),
            pltpu.VMEM((K * C + 8, HALF), F32),
            pltpu.VMEM((3, 4, 4, LONG, HALF), I16),
            pltpu.VMEM((3, 4, 4, LONG, HALF), I16),
            pltpu.VMEM((3, 4, LONG, HALF), I16),
            pltpu.VMEM((3, 4, LONG, HALF), I16),
            pltpu.VMEM((4, LONG, HALF), I16),
            pltpu.VMEM((3, LONG, HALF), I16),
            pltpu.VMEM((LONG, HALF), F32),
            pltpu.VMEM((LONG, HALF), F32),
            pltpu.VMEM((56, HALF), F32),
            pltpu.VMEM((56, HALF), F32),
            dma((4,)), dma((2, 2, 2)), dma((2, 2, 2)), dma((2, 3, 2, 2)), dma((2, 3, 2, 2)), dma((K,)), dma((K,)),
            dma((3, 4)), dma((3, 4)), dma((3,)), dma((3,)), dma((4,)), dma((3,)), dma((2,)),
        ],
        compiler_params=pltpu.CompilerParams(
            collective_id=0, has_side_effects=True, vmem_limit_bytes=56 << 20
        ),
        cost_estimate=pl.CostEstimate(flops=14_500_000_000, bytes_accessed=8_000_000, transcendentals=0),
    )(fine_feat[0, 0], coarse_grad[0, 0], kernel_map[0, 0].T, counts, weight)
    fine, weight_grad = pl.pallas_call(
        finish,
        out_shape=(
            jax.ShapeDtypeStruct((SLOTS, BLOCK, C), BF16),
            jax.ShapeDtypeStruct((MINE, C), F32),
        ),
        in_specs=[vmem, vmem],
        out_specs=(anywhere, anywhere),
        scratch_shapes=[dma((5,))],
        compiler_params=pltpu.CompilerParams(vmem_limit_bytes=8 << 20),
    )(fine, weight_grad)
    return fine[None, None], weight_grad


def solution(mesh):
    return jax.shard_map(
        local,
        mesh=mesh,
        in_specs=(
            P("gx", "gy", None, None, None),
            P("gx", "gy", None, None, None),
            P("gx", "gy", None, None),
            P("gx", "gy"),
            P(),
        ),
        out_specs=(P("gx", "gy", None, None, None), P(("gx", "gy"), None)),
        check_vma=False,
    )
```
